256 devices in a mesh: enc: 8 (over z), rep: 4 (over x), seq: 8 (over y, core).
Axes of the slice: x: 4, y: 4, z: 8, core: 2. Of those that a mesh axis runs over, the one named last changes fastest.
Arguments:
- queries: bfloat16 [65536, 3072], P(('rep', 'seq'), 'enc'), may hold values from -6 to 6
- text: bfloat16 [16, 512, 5120], P('rep', ('enc', 'seq')), may hold values from -6 to 6
- kv_weight: bfloat16 [5120, 2, 3072], P(None, None, 'enc'), may hold values from -0.078125 to 0.078125
- query_gain: float32 [3072], P('enc'), may hold values from 1 to 2.6
- key_gain: float32 [3072], P('enc'), may hold values from 1 to 2.6
- prompt_len: int32 [16], replicated, may hold values from 1 to 512, 4096 in all
- served: int32 [16], replicated, may hold values from 0 to 15, each once
- frame_slot: int32 [4, 128], P('rep', 'seq'), may hold values from 0 to 3, never falling along the last dimension, each value on 1 to 64 neighbouring positions
Outputs:
- attended: bfloat16 [65536, 3072], P(('rep', 'seq'), 'enc')
The draws below stay inside these ranges and needn't reach their ends.
Inputs may be any that keep to these rules, and one draw needn't show every extreme that they name: `prompt_len`: the largest length is exactly 512. `served`: each tenant appears exactly once. `frame_slot`: along each replica's row the value never falls; every one of the 4 positions holds 1 to 64 frame blocks.
All inputs are finite; a program needn't handle non-finite values.
Results may differ from the reference program's by a relative error of at most 0.0099.
Values may be sent and summed in bfloat16 or wider, within the bound.
No kernel may reach another device: no remote copies, remote signals or barrier semaphores. Data moves between devices by JAX's collectives and lax.ppermute only.
A program may use at most 128 MiB of HBM per device.

```python
import math
import jax
import jax.numpy as jnp
import numpy as np
from jax import lax

TD = 5120
HD = 128
HEADS = 24
PMAX = 512
TEN_REP = 4
FRAME = 128
TENANTS = 16
VT = 16384
FRAMES = 128
N_REP = 4


def levels(rng, shape, split, smallest, high):
    def one(dim, shards_of):
        draws = jax.random.uniform(jax.random.fold_in(jax.random.fold_in(rng, 6), dim), (shards_of,), jnp.float32, smallest / len(split), high / len(split))
        return jnp.repeat(jnp.exp(draws), shape[dim] // shards_of).reshape((-1,) + (1,) * (len(shape) - dim - 1))

    level = one(*split[0])
    for cut in split[1:]:
        level = level * one(*cut)
    return level


def split_up(number_of, total, limit, slope):
    loads = [(1 << 20) // math.isqrt(rank ** slope) + 1 for rank in range(2, number_of + 1)]
    surplus, counts = total - limit - (number_of - 1), [1] * (number_of - 1)
    while surplus > 0:
        free = [i for i in range(number_of - 1) if counts[i] < limit]
        pool, budget = sum([loads[i] for i in free]), surplus
        for i in free:
            extra = min(limit - counts[i], max(1, budget * loads[i] // pool), surplus)
            counts[i] = counts[i] + extra
            surplus = surplus - extra
    return np.array([limit] + counts)


def uneven_parts(own_key, number_of, total, reach, skew):
    if number_of == 2:
        one = jax.random.randint(own_key, (), max(1, total - reach), min(reach, total - 1) + 1)
        return jnp.stack([one, total - one])
    tallies = jnp.asarray(split_up(number_of, total, reach, skew), jnp.int32)
    couples = (number_of - 1) // 2
    source_of, receiver = tallies[1:1 + 2 * couples:2], tallies[2:2 + 2 * couples:2]
    margin = jnp.minimum(source_of - 1, reach - receiver)
    shifted = jax.random.randint(jax.random.fold_in(own_key, 1), (couples,), 0, 1 << 20) % (margin + 1)
    tallies = tallies.at[1:1 + 2 * couples:2].set(source_of - shifted).at[2:2 + 2 * couples:2].set(receiver + shifted)
    return tallies[jax.random.permutation(jax.random.fold_in(own_key, 2), number_of)]


def gaussian(stream_key, extent, scale, reach, pieces=(), kind=jnp.bfloat16):
    factor_of = levels(stream_key, extent, pieces, -0.22, 0.18) if pieces else 1.0
    entries = jax.random.normal(stream_key, extent, jnp.float32) * scale * factor_of
    return jnp.minimum(jnp.maximum(entries, -reach), reach).astype(kind)


def setup_inputs(seed: int = 0) -> dict:
    key_list = jax.random.split(jax.random.key(seed), 9)
    return {
        "queries": gaussian(key_list[0], (N_REP * VT, HEADS * HD), 1.0, 6.0, ((0, 32), (1, 8))),
        "text": gaussian(key_list[1], (TENANTS, PMAX, TD), 1.0, 6.0, ((0, 4), (1, 64))),
        "kv_weight": gaussian(key_list[2], (TD, 2, HEADS * HD), TD ** -0.5, 0.078125, ((2, 8),)),
        "query_gain": jnp.clip(jnp.exp(math.log(2.6) - 0.9555114 * jax.random.uniform(key_list[3], (HEADS * HD,), jnp.float32) ** levels(key_list[3], (HEADS * HD,), ((0, 8),), -0.2, 0.2)), 1.0, 2.6),
        "key_gain": jnp.clip(jnp.exp(math.log(2.6) - 0.9555114 * jax.random.uniform(key_list[4], (HEADS * HD,), jnp.float32) ** levels(key_list[4], (HEADS * HD,), ((0, 8),), -0.2, 0.2)), 1.0, 2.6),
        "prompt_len": uneven_parts(key_list[5], TENANTS, TENANTS * PMAX // 2, PMAX, 2).astype(jnp.int32),
        "served": jax.random.permutation(key_list[6], TENANTS).astype(jnp.int32),
        "frame_slot": jax.vmap(lambda own: jnp.searchsorted(jnp.cumsum(uneven_parts(own, TEN_REP, FRAMES, FRAMES // 2, 2)), jnp.arange(FRAMES), side="right"))(jax.random.split(key_list[7], N_REP)).reshape((N_REP, FRAMES)).astype(jnp.int32),
    }


def full_norm(values_in, gain):
    square = lax.optimization_barrier(jnp.mean(values_in * values_in, axis=-1, keepdims=True))
    return values_in * lax.rsqrt(square + 1e-06) * gain

def reference(queries, text, kv_weight, query_gain, key_gain, prompt_len, served, frame_slot):
    flat_weight = kv_weight.reshape(TD, 2 * HEADS * HD)
    projected = jnp.dot(text.reshape(TENANTS * PMAX, TD), flat_weight, preferred_element_type=jnp.float32)
    projected = projected.reshape(TENANTS, PMAX, 2, HEADS * HD)
    keys = full_norm(projected[:, :, 0], key_gain).astype(jnp.bfloat16)
    values = projected[:, :, 1].astype(jnp.bfloat16)
    table = served.reshape(N_REP, TEN_REP)
    tenant_of = jnp.take_along_axis(table, frame_slot.astype(jnp.int32), axis=1).reshape(-1).astype(jnp.int32)
    frame_queries = queries.reshape(N_REP * FRAMES, FRAME, HEADS * HD)
    positions = jnp.arange(PMAX, dtype=jnp.int32)

    def one_frame(frame_items):
        query_rows, tenant = frame_items
        scaled = (full_norm(query_rows.astype(jnp.float32), query_gain) * HD ** (-0.5)).astype(jnp.bfloat16)
        scaled = lax.optimization_barrier(scaled)
        scaled = scaled.astype(jnp.float32).reshape(FRAME, HEADS, HD)
        keys_here = keys[tenant].astype(jnp.float32).reshape(PMAX, HEADS, HD)
        values_here = values[tenant].astype(jnp.float32).reshape(PMAX, HEADS, HD)
        scores = jnp.einsum('qhd,khd->hqk', scaled, keys_here)
        live = positions < prompt_len[tenant]
        raised = jnp.where(live[None, None, :], jnp.exp(scores), jnp.zeros_like(scores))
        probs = (raised / lax.optimization_barrier(jnp.sum(raised, axis=-1, keepdims=True))).astype(jnp.bfloat16)
        probs = lax.optimization_barrier(probs)
        mixed = jnp.einsum('hqk,khd->qhd', probs.astype(jnp.float32), values_here)
        return mixed.reshape(FRAME, HEADS * HD).astype(jnp.bfloat16)
    attended = lax.map(one_frame, (frame_queries, tenant_of))
    return attended.reshape(N_REP * VT, HEADS * HD)
```

```python
import functools

import jax
import jax.numpy as jnp
from jax import lax
from jax.experimental import pallas as pl
from jax.experimental.pallas import tpu as pltpu
from jax.sharding import PartitionSpec as P

HD = 128
FRAME = 128
V_DOWN = 2.0 ** -12
HIGH = 48 * 1024 * 1024


def ring(n, k):
    return [(i, (i + k) % n) for i in range(n)]


def pick_kernel(code, text, ahead, behind, far_a, far_b, out_a, out_b, sem):
    half = out_a.shape[0]
    copies = []
    for j in range(2 * half):
        target = (out_a if j < half else out_b).at[j % half]
        shift, slot = code[j] // 4, code[j] % 4

        def send(source, index, target=target, j=j):
            pltpu.make_async_copy(source.at[index], target, sem.at[j]).start()

        pl.when(shift == 0)(functools.partial(send, text, slot))
        pl.when(shift == 1)(functools.partial(send, behind, slot))
        pl.when((shift == 2) & (slot < 2))(functools.partial(send, far_a, slot % 2))
        pl.when((shift == 2) & (slot >= 2))(functools.partial(send, far_b, slot % 2))
        pl.when(shift == 3)(functools.partial(send, ahead, slot))
        copies.append(pltpu.make_async_copy(text.at[0], target, sem.at[j]))
    for copy in copies:
        copy.wait()


def pick(code, text, ahead, behind, far_a, far_b):
    n, rows, width = text.shape
    half = jax.ShapeDtypeStruct((n // 2, rows, width), text.dtype)
    return pl.pallas_call(
        pick_kernel,
        out_shape=(half, half),
        in_specs=[pl.BlockSpec(memory_space=pltpu.SMEM)] + [pl.BlockSpec(memory_space=pl.ANY)] * 5,
        out_specs=[pl.BlockSpec(memory_space=pl.ANY)] * 2,
        scratch_shapes=[pltpu.SemaphoreType.DMA((n,))],
        name="pick",
    )(code, text, ahead, behind, far_a, far_b)


def project_kernel(info, *refs):
    blocks_a, blocks_b, weight = refs[:8], refs[8:16], refs[16]
    keys_out, values_out, total = refs[17:]
    step = pl.program_id(0)
    pieces = []
    for ref in blocks_a + blocks_b:
        for t in range(2):
            pieces.append(ref[t])
    rows = jnp.concatenate(pieces, axis=0)
    part = jnp.dot(rows, weight[...], preferred_element_type=jnp.float32)

    @pl.when(step == 0)
    def _():
        total[...] = part

    @pl.when(step > 0)
    def _():
        total[...] += part

    @pl.when(step == pl.num_programs(0) - 1)
    def _():
        columns = keys_out.shape[-1]
        enc, seq = info[0], info[1]
        place = lax.broadcasted_iota(jnp.int32, (8, columns), 0)
        row = 0
        for offsets, base in (((0, -1, -2, -3, -4, 1, 2, 3), 0), ((0, -1, -2, -3, 1, 2, 3, 4), 2)):
            for offset in offsets:
                plane = lax.rem(enc + offset + 8, 8)
                for t in range(2):
                    both = total[row * 8:row * 8 + 8, :]
                    row += 1
                    live = plane * 64 + seq * 8 + place < info[2 + base + t]
                    keys_out[base + t, plane] = both[:, :columns]
                    values_out[base + t, plane] = jnp.where(
                        live, both[:, columns:] * V_DOWN, 0.0
                    ).astype(values_out.dtype)


def project(info, blocks_a, blocks_b, weight):
    width, both = weight.shape
    chunk = 512
    columns = both // 2
    block = pl.BlockSpec((2, 8, chunk), lambda k: (0, 0, k))
    whole = pl.BlockSpec((4, 8, 8, columns), lambda k: (0, 0, 0, 0))
    return pl.pallas_call(
        project_kernel,
        out_shape=(
            jax.ShapeDtypeStruct((4, 8, 8, columns), jnp.float32),
            jax.ShapeDtypeStruct((4, 8, 8, columns), jnp.bfloat16),
        ),
        grid=(width // chunk,),
        in_specs=[pl.BlockSpec(memory_space=pltpu.SMEM)]
        + [block] * 16
        + [pl.BlockSpec((chunk, both), lambda k: (k, 0))],
        out_specs=[whole, whole],
        scratch_shapes=[pltpu.VMEM((256, both), jnp.float32)],
        compiler_params=pltpu.CompilerParams(vmem_limit_bytes=HIGH),
        cost_estimate=pl.CostEstimate(
            flops=2 * 256 * width * both, bytes_accessed=2 * (256 * width + width * both), transcendentals=0
        ),
        name="project",
    )(info, *blocks_a, *blocks_b, weight)


def attend_kernel(info, bounds, queries, *refs):
    key_parts, value_parts = refs[:10], refs[10:20]
    out = refs[20]
    q_buf, o_buf, k_buf, v_buf, sem = refs[21:]
    seq, heads = info[1], queries.shape[1] // HD
    total_rows = queries.shape[0]

    def spots(core):
        y, c = seq // 2, (seq % 2 + core) % 2
        return [(2 * lax.rem(y + d + 4, 4) + c, lo, n) for d, lo, n in ((0, 0, 4), (-1, 0, 4), (1, 0, 4), (2, 0, 2), (2, 2, 2))]

    where = spots(0) + spots(1)
    copies = [pltpu.make_async_copy(queries, q_buf.at[pl.ds(0, total_rows)], sem.at[0])]
    for n, (spot, lo, count) in enumerate(where):
        target = pl.ds(pl.multiple_of(spot * 64, 64), 64)
        copies.append(
            pltpu.make_async_copy(key_parts[n], k_buf.at[pl.ds(lo, count), target], sem.at[1 + 4 * n])
        )
        for h in range(heads):
            copies.append(
                pltpu.make_async_copy(
                    value_parts[n].at[:, :, pl.ds(h * HD, HD)],
                    v_buf.at[h, pl.ds(lo, count), target, pl.ds(0, HD)],
                    sem.at[2 + 4 * n + h],
                )
            )
    for copy in copies:
        copy.start()
    q_buf[total_rows:] = jnp.zeros((q_buf.shape[0] - total_rows, q_buf.shape[1]), q_buf.dtype)
    spot = lax.broadcasted_iota(jnp.int32, (512, HD), 0)
    position = (spot // 8) % 8 * 64 + spot // 64 * 8 + spot % 8
    for t in range(4):
        live = jnp.where(position < info[2 + t], 1.0, 0.0).astype(v_buf.dtype)
        for h in range(heads):
            v_buf[h, t, :, HD:] = live
    for copy in copies:
        copy.wait()

    for t in range(4):
        first, last = bounds[t], bounds[t + 1]

        def one(i, carry, t=t, first=first):
            rows = pl.ds(pl.multiple_of((first + 2 * i) * FRAME, FRAME), 2 * FRAME)
            for h in range(heads):
                lanes = slice(h * HD, (h + 1) * HD)
                scores = lax.dot_general(
                    q_buf[rows, lanes], k_buf[t, :, lanes], (((1,), (1,)), ((), ())),
                    preferred_element_type=jnp.float32,
                )
                raised = jnp.exp(scores).astype(jnp.bfloat16)
                mixed = jnp.dot(raised, v_buf[h, t], preferred_element_type=jnp.float32)
                o_buf[rows, lanes] = (
                    mixed[:, :HD] * (1.0 / mixed[:, HD:]) * (1.0 / V_DOWN)
                ).astype(o_buf.dtype)
            return carry

        lax.fori_loop(0, (last - first + 1) // 2, one, 0)
    copy = pltpu.make_async_copy(o_buf.at[pl.ds(0, total_rows)], out, sem.at[0])
    copy.start()
    copy.wait()


def attend(info, bounds, queries, key_parts, value_parts):
    rows, columns = queries.shape
    heads = columns // HD
    smem = pl.BlockSpec(memory_space=pltpu.SMEM)
    hbm = pl.BlockSpec(memory_space=pl.ANY)
    return pl.pallas_call(
        attend_kernel,
        out_shape=jax.ShapeDtypeStruct((rows, columns), queries.dtype),
        in_specs=[smem, smem] + [hbm] * 21,
        out_specs=hbm,
        scratch_shapes=[
            pltpu.VMEM((rows + FRAME, columns), queries.dtype),
            pltpu.VMEM((rows + FRAME, columns), queries.dtype),
            pltpu.VMEM((4, 512, columns), queries.dtype),
            pltpu.VMEM((heads, 4, 512, 2 * HD), queries.dtype),
            pltpu.SemaphoreType.DMA((64,)),
        ],
        compiler_params=pltpu.CompilerParams(vmem_limit_bytes=HIGH),
        cost_estimate=pl.CostEstimate(flops=4 * rows * columns * 512, bytes_accessed=4 * rows * columns, transcendentals=0),
        name="attend",
    )(info, bounds, queries, *key_parts, *value_parts)


def spread(piece):
    up = [(s, (s + 2) % 8) for s in range(8)]
    down = [(s, (s - 2) % 8) for s in range(8)]
    core = [(s, s ^ 1) for s in range(8)]
    ahead = lax.ppermute(piece, "seq", up)
    behind = lax.ppermute(piece, "seq", down)
    far_a = lax.ppermute(ahead[:2], "seq", up)
    far_b = lax.ppermute(behind[2:], "seq", down)
    mine = [piece, ahead, behind, far_a, far_b]
    return mine + [lax.ppermute(part, "seq", core) for part in mine]


def enc_total(square):
    for d in (1, 2, 4):
        square = square + lax.ppermute(square, "enc", [(i, i ^ d) for i in range(8)])
    return square


def local(queries, text, kv_weight, query_gain, key_gain, prompt_len, served, frame_slot):
    columns = queries.shape[1]
    full_width = columns * 8
    enc, rep, seq = (lax.axis_index(a) for a in ("enc", "rep", "seq"))

    ahead = lax.ppermute(text, "rep", ring(4, 1))
    behind = lax.ppermute(text, "rep", ring(4, -1))
    far_a = lax.ppermute(ahead[:2], "rep", ring(4, 1))
    far_b = lax.ppermute(behind[2:], "rep", ring(4, -1))
    mine = lax.dynamic_slice_in_dim(served, rep * 4, 4)
    code = (mine // 4 - rep + 4) % 4 * 4 + mine % 4
    info = jnp.concatenate([jnp.stack([enc, seq]).astype(jnp.int32), prompt_len[mine]])
    bounds = jnp.sum(frame_slot.reshape(1, -1) < jnp.arange(5, dtype=jnp.int32)[:, None], axis=1, dtype=jnp.int32)

    query_float = queries.astype(jnp.float32)
    query_total = enc_total(jnp.sum(query_float * query_float, axis=-1))
    query_scale = lax.rsqrt(query_total / full_width + 1e-06)
    scaled = (query_float * query_scale[:, None] * query_gain * HD ** (-0.5)).astype(jnp.bfloat16)

    weight = kv_weight.reshape(kv_weight.shape[0], 2 * columns)

    part_a, part_b = pick(code, text, ahead, behind, far_a, far_b)
    up, down = ring(8, 1), ring(8, -1)
    a_up, a_down, b_up, b_down = [part_a], [part_a], [part_b], [part_b]
    for i in range(4):
        a_up.append(lax.ppermute(a_up[-1], "enc", up))
        if i < 3:
            a_down.append(lax.ppermute(a_down[-1], "enc", down))
            b_up.append(lax.ppermute(b_up[-1], "enc", up))
        b_down.append(lax.ppermute(b_down[-1], "enc", down))

    raw_keys, values = project(info, a_up + a_down[1:], b_up + b_down[1:], weight)
    raw_keys = raw_keys.reshape(4, 64, columns)
    value_parts = spread(values.reshape(4, 64, columns))
    key_total = enc_total(jnp.sum(raw_keys * raw_keys, axis=-1))
    key_scale = lax.rsqrt(key_total / full_width + 1e-06)
    place = jnp.arange(64, dtype=jnp.int32)
    position = place // 8 * 64 + seq * 8 + place % 8
    live = position[None, :] < info[2:, None]
    keys = jnp.where(
        live[:, :, None], raw_keys * key_scale[:, :, None] * key_gain, 0.0
    ).astype(jnp.bfloat16)
    key_parts = spread(keys)
    return attend(info, bounds, scaled, key_parts, value_parts)


def solution(mesh):
    placed = (
        P(("rep", "seq"), "enc"),
        P("rep", ("enc", "seq"), None),
        P(None, None, "enc"),
        P("enc"),
        P("enc"),
        P(),
        P(),
        P("rep", "seq"),
    )
    return jax.shard_map(
        local, mesh=mesh, in_specs=placed, out_specs=P(("rep", "seq"), "enc"), check_vma=False
    )
```

```python
import functools
import math

import jax
import jax.numpy as jnp
from jax import lax
from jax.experimental import pallas as pl
from jax.experimental.pallas import tpu as pltpu
from jax.sharding import PartitionSpec as P

HD = 128
FRAME = 128
V_DOWN = 2.0 ** -12
MIB = 1024 * 1024
CHUNK = 512
GROUP = 4
PLANES = (0, -1, -2, -3, 4, 1, 2, 3)

SMEM = pl.BlockSpec(memory_space=pltpu.SMEM)
VMEM = pl.BlockSpec(memory_space=pltpu.VMEM)
HBM = pl.BlockSpec(memory_space=pl.ANY)


def ring(n, k):
    return [(i, (i + k) % n) for i in range(n)]


Y_UP = [(s, (s + 2) % 8) for s in range(8)]
Y_DOWN = [(s, (s - 2) % 8) for s in range(8)]
CORE = [(s, s ^ 1) for s in range(8)]


def pick_kernel(code, text, ahead, behind, far_a, far_b, *refs):
    out, sem = refs[-2:]
    rows, width = text.shape[1:]
    copies = []
    for j in range(out.shape[0]):
        target = out.at[j] if out.shape[2] == width else out.at[j, :, pl.ds(0, width)]
        shift, slot = code[j] // 4, code[j] % 4

        def send(source, index, target=target, j=j):
            pltpu.make_async_copy(source.at[index], target, sem.at[j]).start()

        pl.when(shift == 0)(functools.partial(send, text, slot))
        pl.when(shift == 1)(functools.partial(send, behind, slot))
        pl.when((shift == 2) & (slot < 2))(functools.partial(send, far_a, slot % 2))
        pl.when((shift == 2) & (slot >= 2))(functools.partial(send, far_b, slot % 2))
        pl.when(shift == 3)(functools.partial(send, ahead, slot))
        copies.append(pltpu.make_async_copy(text.at[0], target, sem.at[j]))
    if out.shape[2] > width:
        square = refs[0]
        for j in range(2):
            part = square[j * rows:(j + 1) * rows, :]
            upper = part.astype(out.dtype)
            out[j, :, width:] = upper
            out[2 + j, :, width:] = (part - upper.astype(jnp.float32)).astype(out.dtype)
    for copy in copies:
        copy.wait()


def pick(code, text, ahead, behind, far_a, far_b, square=None, *first):
    extra = 0 if square is None else HD
    first = first if square is None else (square,) + first
    n, rows, width = text.shape
    return pl.pallas_call(
        pick_kernel,
        out_shape=jax.ShapeDtypeStruct((n, rows, width + extra), text.dtype),
        in_specs=[SMEM] + [HBM] * 5 + [VMEM] * (extra // HD) + [HBM] * (len(first) - extra // HD),
        out_specs=VMEM,
        scratch_shapes=[pltpu.SemaphoreType.DMA((text.shape[0],))],
        compiler_params=pltpu.CompilerParams(vmem_limit_bytes=4 * MIB),
        name="pick",
    )(code, text, ahead, behind, far_a, far_b, *first)


def project_kernel(info, gain, *refs):
    n = len(PLANES)
    halves, weight = (refs[:n], refs[n:2 * n]), refs[2 * n]
    out, squares, query_total, row_buf, weight_buf, total, raw, row_sem, weight_sem = refs[-9:]
    width = weight.shape[0] // 2
    steps = [(half, k) for half in range(2) for k in range(0, width, CHUNK)]
    loads = [
        pltpu.make_async_copy(weight.at[pl.ds(half * width + k, CHUNK)], weight_buf.at[i], weight_sem.at[i])
        for i, (half, k) in enumerate(steps)
    ]
    fetches = [
        [
            pltpu.make_async_copy(
                block, row_buf.at[half, pl.ds(32 * i, 32), pl.ds(0, block.shape[1])], row_sem.at[half, i]
            )
            for i, block in enumerate(blocks)
        ]
        for half, blocks in enumerate(halves)
    ]
    for copy in fetches[0] + loads[:2] + fetches[1] + loads[2:]:
        copy.start()
    for i, (half, k) in enumerate(steps):
        if k == 0:
            for fetch in fetches[half]:
                fetch.wait()
        loads[i].wait()
        part = jnp.dot(row_buf[half, :, k:k + CHUNK], weight_buf[i], preferred_element_type=jnp.float32)
        if i == 0:
            total[...] = part
        else:
            total[...] += part
    riders = [row_buf[1, 32 * i:32 * i + 32, width:].astype(jnp.float32) for i in range(n)]
    query_total[...] = sum(rider[:16] + rider[16:] for rider in riders)
    columns = out.shape[-1] // 2
    enc, seq = info[0], info[1]
    place = lax.broadcasted_iota(jnp.int32, (8, columns), 0)
    for i, offset in enumerate(PLANES):
        plane = lax.rem(enc + offset + 8, 8)
        for t in range(4):
            both = total[32 * i + 8 * t:32 * i + 8 * t + 8, :]
            live = plane * 64 + seq * 8 + place < info[2 + t]
            raw[t, plane] = both[:, :columns]
            out[t, plane, :, :columns] = (both[:, :columns] * gain[...]).astype(out.dtype)
            out[t, plane, :, columns:] = jnp.where(
                live, both[:, columns:] * V_DOWN, 0.0
            ).astype(out.dtype)
    square = raw[...].reshape(256, columns)
    square = square * square
    upper = square.astype(jnp.bfloat16)
    lower = (square - upper.astype(jnp.float32)).astype(jnp.bfloat16)
    ones = jnp.ones((squares.shape[0], columns), jnp.bfloat16)
    across = (((1,), (1,)), ((), ()))
    squares[...] = lax.dot_general(
        ones, upper, across, preferred_element_type=jnp.float32
    ) + lax.dot_general(ones, lower, across, preferred_element_type=jnp.float32)


def project(info, gain, blocks, weight):
    width, both = weight.shape
    return pl.pallas_call(
        project_kernel,
        out_shape=(
            jax.ShapeDtypeStruct((4, 8, 8, both), jnp.bfloat16),
            jax.ShapeDtypeStruct((64, 256), jnp.float32),
            jax.ShapeDtypeStruct((16, HD), jnp.float32),
        ),
        in_specs=[SMEM, VMEM] + [HBM] * (len(blocks) + 1),
        out_specs=[VMEM] * 3,
        scratch_shapes=[
            pltpu.VMEM((2, 256, width // 2 + HD), jnp.bfloat16),
            pltpu.VMEM((width // CHUNK, CHUNK, both), jnp.bfloat16),
            pltpu.VMEM((256, both), jnp.float32),
            pltpu.VMEM((4, 8, 8, both // 2), jnp.float32),
            pltpu.SemaphoreType.DMA((2, len(PLANES))),
            pltpu.SemaphoreType.DMA((width // CHUNK,)),
        ],
        compiler_params=pltpu.CompilerParams(vmem_limit_bytes=56 * MIB),
        cost_estimate=pl.CostEstimate(
            flops=2 * 256 * width * both, bytes_accessed=2 * (256 * width + width * both), transcendentals=0
        ),
        name="project",
    )(info, gain, *blocks, weight)


def cut_kernel(ahead, behind, squares, out_a, out_b, total, sem):
    count = out_a.shape[0]
    copies = [
        pltpu.make_async_copy(ahead.at[pl.ds(0, count)], out_a, sem.at[0]),
        pltpu.make_async_copy(behind.at[pl.ds(count, count)], out_b, sem.at[1]),
    ]
    for copy in copies:
        copy.start()
    total[...] = jnp.sum(squares[...].reshape(8, 8, 256), axis=0)
    for copy in copies:
        copy.wait()


def cut(ahead, behind, squares):
    n, rows, columns = ahead.shape
    half = jax.ShapeDtypeStruct((n // 2, rows, columns), ahead.dtype)
    return pl.pallas_call(
        cut_kernel,
        out_shape=(half, half, jax.ShapeDtypeStruct((8, 256), jnp.float32)),
        in_specs=[HBM, HBM, VMEM],
        out_specs=[VMEM] * 3,
        scratch_shapes=[pltpu.SemaphoreType.DMA((2,))],
        compiler_params=pltpu.CompilerParams(vmem_limit_bytes=4 * MIB),
        name="cut",
    )(ahead, behind, squares)


def attend_kernel(width, info, bounds, queries, gain, query_total, key_total, *refs):
    parts, out = refs[:10], refs[10]
    raw_buf, q_buf, o_buf, k_buf, v_buf, scale_buf, sem, query_sem = refs[11:]
    seq, heads = info[1], queries.shape[1] // HD
    columns = heads * HD
    frames = queries.shape[0] // FRAME
    load = pltpu.make_async_copy(queries, raw_buf, query_sem)
    load.start()

    def piece_seq(piece):
        y, c = seq // 2, seq % 2
        kind = piece % 4
        shift = jnp.where(kind == 0, 0, jnp.where(kind == 1, 3, jnp.where(kind == 2, 1, 2)))
        return 2 * ((y + shift) % 4) + (c + piece // 4) % 2

    def position(shape, axis):
        key = lax.broadcasted_iota(jnp.int32, shape, axis)
        return key // 8 % 8 * 64 + piece_seq(key // 64) * 8 + key % 8

    down, across = position((512, HD), 0), position((1, 512), 1)
    totals = [key_total[pl.ds(piece_seq(p), 1), :] for p in range(8)]
    scales = [lax.rsqrt(total / width + 1e-06) * math.log2(math.e) for total in totals]
    for t in range(4):
        live = jnp.where(down < info[2 + t], 1.0, 0.0).astype(v_buf.dtype)
        row = jnp.concatenate([scale[:, t * 64:t * 64 + 64] for scale in scales], axis=1)
        scale_buf[t:t + 1, :] = jnp.where(across < info[2 + t], row, 0.0)
        for p in range(8):
            own = parts[p // 4 * 5 + p % 4]
            piece, slot = (own, t) if p % 4 < 3 else (parts[p // 4 * 5 + 3 + t // 2], t % 2)
            spot = slice(64 * p, 64 * p + 64)
            k_buf[t, spot, :] = piece[slot, :, :columns]
            for h in range(heads):
                v_buf[h, t, spot, :HD] = piece[slot, :, columns + h * HD:columns + (h + 1) * HD]
        for h in range(heads):
            v_buf[h, t, :, HD:] = live

    query_scale = jnp.transpose(lax.rsqrt(query_total[...] / width + 1e-06))
    load.wait()
    for f in range(frames):
        rows = slice(f * FRAME, (f + 1) * FRAME)
        q_buf[rows, :] = (
            raw_buf[rows, :].astype(jnp.float32) * query_scale[:, f:f + 1] * gain[...] * HD ** (-0.5)
        ).astype(q_buf.dtype)

    def frame_copy(f):
        rows = pl.ds(pl.multiple_of(f * FRAME, FRAME), FRAME)
        return pltpu.make_async_copy(o_buf.at[rows], out.at[rows], sem.at[f])

    for t in range(4):
        first, last = bounds[t], bounds[t + 1]

        def one(i, carry, t=t, first=first, last=last):
            frame = first + GROUP * i
            base = jnp.minimum(frame, frames - GROUP)
            rows = pl.ds(pl.multiple_of(base * FRAME, FRAME), GROUP * FRAME)
            places = [
                pl.ds(pl.multiple_of(jnp.where(base + g < frame, frames, base + g) * FRAME, FRAME), FRAME)
                for g in range(GROUP)
            ]
            for h in range(heads):
                lanes = slice(h * HD, (h + 1) * HD)
                scores = lax.dot_general(
                    q_buf[rows, lanes], k_buf[t, :, lanes], (((1,), (1,)), ((), ())),
                    preferred_element_type=jnp.float32,
                )
                raised = jnp.exp2(scores * scale_buf[t:t + 1, :]).astype(jnp.bfloat16)
                mixed = jnp.dot(raised, v_buf[h, t], preferred_element_type=jnp.float32)
                result = (mixed[:, :HD] * (1.0 / mixed[:, HD:]) * (1.0 / V_DOWN)).astype(o_buf.dtype)
                for g, place in enumerate(places):
                    o_buf[place, lanes] = result[g * FRAME:(g + 1) * FRAME]
            for g in range(GROUP):

                @pl.when(frame + g < last)
                def _(g=g):
                    frame_copy(frame + g).start()

            return carry

        lax.fori_loop(0, (last - first + GROUP - 1) // GROUP, one, 0)
    for f in range(frames):
        frame_copy(f).wait()


def attend(width, info, bounds, queries, gain, query_total, key_total, parts):
    rows, columns = queries.shape
    return pl.pallas_call(
        functools.partial(attend_kernel, width),
        out_shape=jax.ShapeDtypeStruct((rows, columns), queries.dtype),
        in_specs=[SMEM, SMEM, HBM] + [VMEM] * 13,
        out_specs=HBM,
        scratch_shapes=[
            pltpu.VMEM((rows, columns), queries.dtype),
            pltpu.VMEM((rows, columns), queries.dtype),
            pltpu.VMEM((rows + FRAME, columns), queries.dtype),
            pltpu.VMEM((4, 512, columns), queries.dtype),
            pltpu.VMEM((columns // HD, 4, 512, 2 * HD), queries.dtype),
            pltpu.VMEM((8, 512), jnp.float32),
            pltpu.SemaphoreType.DMA((rows // FRAME,)),
            pltpu.SemaphoreType.DMA,
        ],
        compiler_params=pltpu.CompilerParams(vmem_limit_bytes=20 * MIB),
        cost_estimate=pl.CostEstimate(flops=4 * rows * columns * 512, bytes_accessed=4 * rows * columns, transcendentals=0),
        name="attend",
    )(info, bounds, queries, gain, query_total, key_total, *parts)


def local(queries, text, kv_weight, query_gain, key_gain, prompt_len, served, frame_slot):
    columns = queries.shape[1]
    full_width = columns * 8
    enc, rep, seq = (lax.axis_index(a) for a in ("enc", "rep", "seq"))
    mine = lax.dynamic_slice_in_dim(served, rep * 4, 4)
    code = (mine // 4 - rep + 4) % 4 * 4 + mine % 4
    info = jnp.concatenate([jnp.stack([enc, seq]).astype(jnp.int32), prompt_len[mine]])
    bounds = jnp.sum(frame_slot.reshape(1, -1) < jnp.arange(5, dtype=jnp.int32)[:, None], axis=1, dtype=jnp.int32)
    query_float = queries.astype(jnp.float32)
    query_square = jnp.sum(query_float * query_float, axis=-1).reshape(-1, HD)
    half = text.shape[2] // 2
    weight = kv_weight.reshape(kv_weight.shape[0], 2 * columns)

    blocks = []
    for n in range(2):
        part = text[:, :, n * half:(n + 1) * half]
        ahead = lax.ppermute(part, "rep", ring(4, 1))
        behind = lax.ppermute(part, "rep", ring(4, -1))
        far_a = lax.ppermute(ahead[:2], "rep", ring(4, 1))
        far_b = lax.ppermute(behind[2:], "rep", ring(4, -1))
        first = (query_square,) if n == 1 else ()
        picked = pick(code, part, ahead, behind, far_a, far_b, *first)
        blocks.append(picked.reshape(32, picked.shape[2]))

    ups, downs = [[b] for b in blocks], [[b] for b in blocks]
    for i in range(4):
        for n in range(2):
            if n == 0 or i < 3:
                ups[n].append(lax.ppermute(ups[n][-1], "enc", ring(8, 1)))
            if n == 1 or i < 3:
                downs[n].append(lax.ppermute(downs[n][-1], "enc", ring(8, -1)))
    held = ups[0] + downs[0][1:] + ups[1] + [downs[1][4]] + downs[1][1:4]
    pair, squares, query_total = project(info, key_gain[None], held, weight)
    pair = pair.reshape(4, 64, 2 * columns)

    ahead = lax.ppermute(pair, "seq", Y_UP)
    behind = lax.ppermute(pair, "seq", Y_DOWN)
    squares = lax.all_to_all(squares, ("enc", "seq"), 0, 0, tiled=True)
    cut_a, cut_b, key_total = cut(ahead, behind, squares)
    far_a = lax.ppermute(cut_a, "seq", Y_UP)
    far_b = lax.ppermute(cut_b, "seq", Y_DOWN)
    parts = [pair, ahead, behind, far_a, far_b]
    parts = parts + [lax.ppermute(part, "seq", CORE) for part in parts]
    return attend(full_width, info, bounds, queries, query_gain[None], query_total, key_total, parts)


def solution(mesh):
    placed = (
        P(("rep", "seq"), "enc"),
        P("rep", ("enc", "seq"), None),
        P(None, None, "enc"),
        P("enc"),
        P("enc"),
        P(),
        P(),
        P("rep", "seq"),
    )
    return jax.shard_map(
        local, mesh=mesh, in_specs=placed, out_specs=P(("rep", "seq"), "enc"), check_vma=False
    )
```

```python
import functools
import math

import jax
import jax.numpy as jnp
from jax import lax
from jax.experimental import pallas as pl
from jax.experimental.pallas import tpu as pltpu
from jax.sharding import PartitionSpec as P

HD = 128
FRAME = 128
V_DOWN = 2.0 ** -12
MIB = 1024 * 1024
CHUNK = 512
GROUP = 4
PLANES = (0, -1, -2, -3, 4, 1, 2, 3)

SMEM = pl.BlockSpec(memory_space=pltpu.SMEM)
VMEM = pl.BlockSpec(memory_space=pltpu.VMEM)
HBM = pl.BlockSpec(memory_space=pl.ANY)


def ring(n, k):
    return [(i, (i + k) % n) for i in range(n)]


Y_UP = [(s, (s + 2) % 8) for s in range(8)]
Y_DOWN = [(s, (s - 2) % 8) for s in range(8)]
Y_FAR = [(s, (s + 4) % 8) for s in range(8)]
CORE = [(s, s ^ 1) for s in range(8)]


def pick_kernel(info, *refs):
    sources, out, sem = refs[:4], refs[-2], refs[-1]
    rows, width = sources[0].shape[1:]
    copies = []
    for j in range(out.shape[0]):
        target = out.at[j] if out.shape[2] == width else out.at[j, :, pl.ds(0, width)]
        step, slot = info[6 + j] // 4, info[6 + j] % 4

        def send(source, index, target=target, j=j):
            pltpu.make_async_copy(source.at[index], target, sem.at[j]).start()

        for i, source in enumerate(sources):
            pl.when(step == i)(functools.partial(send, source, slot))
        copies.append(pltpu.make_async_copy(sources[0].at[0], target, sem.at[j]))
    if out.shape[2] > width:
        square = refs[4]
        for j in range(2):
            part = square[j * rows:(j + 1) * rows, :]
            upper = part.astype(out.dtype)
            out[j, :, width:] = upper
            out[2 + j, :, width:] = (part - upper.astype(jnp.float32)).astype(out.dtype)
    for copy in copies:
        copy.wait()


def pick(info, parts, square=None):
    extra = 0 if square is None else HD
    n, rows, width = parts[0].shape
    return pl.pallas_call(
        pick_kernel,
        out_shape=jax.ShapeDtypeStruct((n, rows, width + extra), parts[0].dtype),
        in_specs=[SMEM] + [HBM] * 4 + [VMEM] * (extra // HD),
        out_specs=VMEM,
        scratch_shapes=[pltpu.SemaphoreType.DMA((n,))],
        compiler_params=pltpu.CompilerParams(vmem_limit_bytes=4 * MIB),
        name="pick",
    )(info, *parts, *([] if square is None else [square]))


def project_kernel(info, gain, *refs):
    n = len(PLANES)
    halves, weight = (refs[:n], refs[n:2 * n]), refs[2 * n]
    out, squares, query_total, weight_buf, total, raw, weight_sem = refs[-7:]
    width = weight.shape[0] // 2
    steps = [(half, k) for half in range(2) for k in range(0, width, CHUNK)]
    loads = [
        pltpu.make_async_copy(weight.at[pl.ds(half * width + k, CHUNK)], weight_buf.at[i], weight_sem.at[i])
        for i, (half, k) in enumerate(steps)
    ]
    for load in loads:
        load.start()
    for i, (half, k) in enumerate(steps):
        rows = jnp.concatenate([block[:, k:k + CHUNK] for block in halves[half]], axis=0)
        loads[i].wait()
        part = jnp.dot(rows, weight_buf[i], preferred_element_type=jnp.float32)
        if i == 0:
            total[...] = part
        else:
            total[...] += part
    riders = [block[:, width:].astype(jnp.float32) for block in halves[1]]
    query_total[...] = sum(rider[:16] + rider[16:] for rider in riders)
    columns = out.shape[-1] // 2
    enc, seq = info[0], info[1]
    place = lax.broadcasted_iota(jnp.int32, (8, columns), 0)
    for i, offset in enumerate(PLANES):
        plane = lax.rem(enc + offset + 8, 8)
        for t in range(4):
            both = total[32 * i + 8 * t:32 * i + 8 * t + 8, :]
            live = plane * 64 + seq * 8 + place < info[2 + t]
            raw[t, plane] = both[:, :columns]
            out[t, plane, :, :columns] = (both[:, :columns] * gain[...][None, :]).astype(out.dtype)
            out[t, plane, :, columns:] = jnp.where(
                live, both[:, columns:] * V_DOWN, 0.0
            ).astype(out.dtype)
    square = raw[...].reshape(256, columns)
    square = square * square
    upper = square.astype(jnp.bfloat16)
    lower = (square - upper.astype(jnp.float32)).astype(jnp.bfloat16)
    ones = jnp.ones((8, columns), jnp.bfloat16)
    across = (((1,), (1,)), ((), ()))
    summed = lax.dot_general(
        ones, upper, across, preferred_element_type=jnp.float32
    ) + lax.dot_general(ones, lower, across, preferred_element_type=jnp.float32)
    for i in range(0, squares.shape[0], 8):
        squares[i:i + 8] = summed.reshape(8, 1, 256)


def project(info, gain, blocks, weight):
    width, both = weight.shape
    return pl.pallas_call(
        project_kernel,
        out_shape=(
            jax.ShapeDtypeStruct((4, 8, 8, both), jnp.bfloat16),
            jax.ShapeDtypeStruct((64, 1, 256), jnp.float32),
            jax.ShapeDtypeStruct((16, HD), jnp.float32),
        ),
        in_specs=[SMEM] + [VMEM] * (len(blocks) + 1) + [HBM],
        out_specs=[VMEM] * 3,
        scratch_shapes=[
            pltpu.VMEM((width // CHUNK, CHUNK, both), jnp.bfloat16),
            pltpu.VMEM((256, both), jnp.float32),
            pltpu.VMEM((4, 8, 8, both // 2), jnp.float32),
            pltpu.SemaphoreType.DMA((width // CHUNK,)),
        ],
        compiler_params=pltpu.CompilerParams(vmem_limit_bytes=48 * MIB),
        cost_estimate=pl.CostEstimate(
            flops=2 * 256 * width * both, bytes_accessed=2 * (256 * width + width * both), transcendentals=0
        ),
        name="project",
    )(info, gain, *blocks, weight)


def total_kernel(piece, squares, out, total, sem):
    copy = pltpu.make_async_copy(piece, out, sem)
    copy.start()
    for i in range(8):
        row = squares[i]
        for plane in range(1, 8):
            row = row + squares[8 * plane + i]
        total[i:i + 1, :] = row
    copy.wait()


def key_sums(piece, squares):
    return pl.pallas_call(
        total_kernel,
        out_shape=(jax.ShapeDtypeStruct(piece.shape, piece.dtype), jax.ShapeDtypeStruct((8, 256), jnp.float32)),
        in_specs=[HBM, VMEM],
        out_specs=[VMEM] * 2,
        scratch_shapes=[pltpu.SemaphoreType.DMA],
        compiler_params=pltpu.CompilerParams(vmem_limit_bytes=4 * MIB),
        name="key_sums",
    )(piece, squares)


def attend_kernel(width, info, bounds, queries, gain, query_total, key_total, *refs):
    parts, out = refs[:8], refs[8]
    raw_buf, q_buf, o_buf, k_buf, v_buf, scale_buf, sem, query_sem = refs[9:]
    seq, heads = info[1], queries.shape[1] // HD
    columns = heads * HD
    frames = queries.shape[0] // FRAME
    load = pltpu.make_async_copy(queries, raw_buf, query_sem)
    load.start()

    def piece_seq(piece):
        y, c = seq // 2, seq % 2
        kind = piece % 4
        shift = jnp.where(kind == 0, 0, jnp.where(kind == 1, 3, jnp.where(kind == 2, 1, 2)))
        return 2 * ((y + shift) % 4) + (c + piece // 4) % 2

    def position(shape, axis):
        key = lax.broadcasted_iota(jnp.int32, shape, axis)
        return key // 8 % 8 * 64 + piece_seq(key // 64) * 8 + key % 8

    down, across = position((512, HD), 0), position((1, 512), 1)
    totals = [key_total[pl.ds(piece_seq(p), 1), :] for p in range(8)]
    scales = [lax.rsqrt(total / width + 1e-06) * math.log2(math.e) for total in totals]
    for t in range(4):
        live = jnp.where(down < info[2 + t], 1.0, 0.0).astype(v_buf.dtype)
        row = jnp.concatenate([scale[:, t * 64:t * 64 + 64] for scale in scales], axis=1)
        scale_buf[t:t + 1, :] = jnp.where(across < info[2 + t], row, 0.0)
        for p in range(8):
            spot = slice(64 * p, 64 * p + 64)
            k_buf[t, spot, :] = parts[p][t, :, :columns]
            for h in range(heads):
                v_buf[h, t, spot, :HD] = parts[p][t, :, columns + h * HD:columns + (h + 1) * HD]
        for h in range(heads):
            v_buf[h, t, :, HD:] = live

    query_scale = jnp.transpose(lax.rsqrt(query_total[...] / width + 1e-06))
    load.wait()
    for f in range(frames):
        rows = slice(f * FRAME, (f + 1) * FRAME)
        q_buf[rows, :] = (
            raw_buf[rows, :].astype(jnp.float32) * query_scale[:, f:f + 1] * gain[...][None, :] * HD ** (-0.5)
        ).astype(q_buf.dtype)

    def frame_copy(f):
        rows = pl.ds(pl.multiple_of(f * FRAME, FRAME), FRAME)
        return pltpu.make_async_copy(o_buf.at[rows], out.at[rows], sem.at[f])

    for t in range(4):
        first, last = bounds[t], bounds[t + 1]

        def one(i, carry, t=t, first=first, last=last):
            frame = first + GROUP * i
            base = jnp.minimum(frame, frames - GROUP)
            rows = pl.ds(pl.multiple_of(base * FRAME, FRAME), GROUP * FRAME)
            places = [
                pl.ds(pl.multiple_of(jnp.where(base + g < frame, frames, base + g) * FRAME, FRAME), FRAME)
                for g in range(GROUP)
            ]
            for h in range(heads):
                lanes = slice(h * HD, (h + 1) * HD)
                scores = lax.dot_general(
                    q_buf[rows, lanes], k_buf[t, :, lanes], (((1,), (1,)), ((), ())),
                    preferred_element_type=jnp.float32,
                )
                raised = jnp.exp2(scores * scale_buf[t:t + 1, :]).astype(jnp.bfloat16)
                mixed = jnp.dot(raised, v_buf[h, t], preferred_element_type=jnp.float32)
                result = (mixed[:, :HD] * (1.0 / mixed[:, HD:]) * (1.0 / V_DOWN)).astype(o_buf.dtype)
                for g, place in enumerate(places):
                    o_buf[place, lanes] = result[g * FRAME:(g + 1) * FRAME]
            for g in range(GROUP):

                @pl.when(frame + g < last)
                def _(g=g):
                    frame_copy(frame + g).start()

            return carry

        lax.fori_loop(0, (last - first + GROUP - 1) // GROUP, one, 0)
    for f in range(frames):
        frame_copy(f).wait()


def attend(width, info, bounds, queries, gain, query_total, key_total, parts):
    rows, columns = queries.shape
    return pl.pallas_call(
        functools.partial(attend_kernel, width),
        out_shape=jax.ShapeDtypeStruct((rows, columns), queries.dtype),
        in_specs=[SMEM, SMEM, HBM] + [VMEM] * 11,
        out_specs=HBM,
        scratch_shapes=[
            pltpu.VMEM((rows, columns), queries.dtype),
            pltpu.VMEM((rows, columns), queries.dtype),
            pltpu.VMEM((rows + FRAME, columns), queries.dtype),
            pltpu.VMEM((4, 512, columns), queries.dtype),
            pltpu.VMEM((columns // HD, 4, 512, 2 * HD), queries.dtype),
            pltpu.VMEM((8, 512), jnp.float32),
            pltpu.SemaphoreType.DMA((rows // FRAME,)),
            pltpu.SemaphoreType.DMA,
        ],
        compiler_params=pltpu.CompilerParams(vmem_limit_bytes=20 * MIB),
        cost_estimate=pl.CostEstimate(flops=4 * rows * columns * 512, bytes_accessed=4 * rows * columns, transcendentals=0),
        name="attend",
    )(info, bounds, queries, gain, query_total, key_total, *parts)


def local(queries, text, kv_weight, query_gain, key_gain, prompt_len, served, frame_slot):
    columns = queries.shape[1]
    full_width = columns * 8
    enc, rep, seq = (lax.axis_index(a) for a in ("enc", "rep", "seq"))
    mine = lax.dynamic_slice_in_dim(served, rep * 4, 4)
    code = (mine // 4 - rep + 4) % 4 * 4 + mine % 4
    info = jnp.concatenate([jnp.stack([enc, seq]).astype(jnp.int32), prompt_len[mine], code])
    bounds = jnp.sum(frame_slot.reshape(1, -1) < jnp.arange(5, dtype=jnp.int32)[:, None], axis=1, dtype=jnp.int32)
    query_float = queries.astype(jnp.float32)
    query_square = jnp.sum(query_float * query_float, axis=-1).reshape(-1, HD)
    half = text.shape[2] // 2
    weight = kv_weight.reshape(kv_weight.shape[0], 2 * columns)

    blocks = []
    for n in range(2):
        part = text[:, :, n * half:(n + 1) * half]
        parts = [part] + [lax.ppermute(part, "rep", ring(4, k)) for k in (-1, 2, 1)]
        picked = pick(info, parts, query_square if n == 1 else None)
        blocks.append(picked.reshape(32, picked.shape[2]))

    ups, downs = [[b] for b in blocks], [[b] for b in blocks]
    for i in range(4):
        for n in range(2):
            if n == 0 or i < 3:
                ups[n].append(lax.ppermute(ups[n][-1], "enc", ring(8, 1)))
            if n == 1 or i < 3:
                downs[n].append(lax.ppermute(downs[n][-1], "enc", ring(8, -1)))
    held = ups[0] + downs[0][1:] + ups[1] + [downs[1][4]] + downs[1][1:4]
    pair, squares, query_total = project(info, key_gain, held, weight)
    pair = pair.reshape(4, 64, 2 * columns)

    squares = lax.all_to_all(squares, ("enc", "seq"), 0, 0, tiled=True)
    ahead, behind, far = (lax.ppermute(pair, "seq", p) for p in (Y_UP, Y_DOWN, Y_FAR))
    far, key_total = key_sums(far, squares)
    parts = [pair, ahead, behind, far]
    parts = parts + [lax.ppermute(part, "seq", CORE) for part in parts]
    return attend(full_width, info, bounds, queries, query_gain, query_total, key_total, parts)


def solution(mesh):
    placed = (
        P(("rep", "seq"), "enc"),
        P("rep", ("enc", "seq"), None),
        P(None, None, "enc"),
        P("enc"),
        P("enc"),
        P(),
        P(),
        P("rep", "seq"),
    )
    return jax.shard_map(
        local, mesh=mesh, in_specs=placed, out_specs=P(("rep", "seq"), "enc"), check_vma=False
    )
```

```python
import functools
import math

import jax
import jax.numpy as jnp
from jax import lax
from jax.experimental import pallas as pl
from jax.experimental.pallas import tpu as pltpu
from jax.sharding import PartitionSpec as P

HD = 128
FRAME = 128
V_DOWN = 2.0 ** -12
MIB = 1024 * 1024
CHUNK = 512
GROUP = 4
RING = 8
PLANES = (0, -1, -2, -3, 4, 1, 2, 3)

SMEM = pl.BlockSpec(memory_space=pltpu.SMEM)
VMEM = pl.BlockSpec(memory_space=pltpu.VMEM)
HBM = pl.BlockSpec(memory_space=pl.ANY)


def ring(n, k):
    return [(i, (i + k) % n) for i in range(n)]


def planes(k):
    return [(i * 8 + s, (i + k * (1 - 2 * (s % 2))) % RING * 8 + s) for i in range(RING) for s in range(8)]


Y_UP = [(s, (s + 2) % 8) for s in range(8)]
Y_DOWN = [(s, (s - 2) % 8) for s in range(8)]
Y_FAR = [(s, (s + 4) % 8) for s in range(8)]
CORE = [(s, s ^ 1) for s in range(8)]


def pick_kernel(info, *refs):
    sources, square = refs[:4], refs[4]
    out_a, out_b, sem = refs[-3:]
    tenants, rows, width = out_a.shape
    copies = []
    for j in range(tenants):
        step, slot = info[6 + j] // 4, info[6 + j] % 4
        for n, target in enumerate((out_a.at[j], out_b.at[j, :, pl.ds(0, width)])):
            span = pl.ds(n * width, width)

            def send(source, index, target=target, span=span, j=j, n=n):
                pltpu.make_async_copy(source.at[index, :, span], target, sem.at[n, j]).start()

            for i, source in enumerate(sources):
                pl.when(step == i)(functools.partial(send, source, slot))
            copies.append(pltpu.make_async_copy(sources[0].at[0, :, span], target, sem.at[n, j]))
    for j in range(2):
        part = square[j * rows:(j + 1) * rows, :]
        upper = part.astype(out_b.dtype)
        out_b[j, :, width:] = upper
        out_b[2 + j, :, width:] = (part - upper.astype(jnp.float32)).astype(out_b.dtype)
    for copy in copies:
        copy.wait()


def pick(info, parts, square, weight):
    n, rows, width = parts[0].shape
    return pl.pallas_call(
        pick_kernel,
        out_shape=(
            jax.ShapeDtypeStruct((n, rows, width // 2), parts[0].dtype),
            jax.ShapeDtypeStruct((n, rows, width // 2 + HD), parts[0].dtype),
        ),
        in_specs=[SMEM] + [HBM] * 4 + [VMEM, HBM],
        out_specs=[VMEM] * 2,
        scratch_shapes=[pltpu.SemaphoreType.DMA((2, n))],
        compiler_params=pltpu.CompilerParams(vmem_limit_bytes=48 * MIB),
        name="pick",
    )(info, *parts, square, weight)


def multiply(blocks, weight, start, total, weight_buf, sem):
    steps = range(weight_buf.shape[0])
    loads = [
        pltpu.make_async_copy(weight.at[pl.ds(start + i * CHUNK, CHUNK)], weight_buf.at[i], sem.at[i])
        for i in steps
    ]
    for load in loads:
        load.start()
    for i in steps:
        rows = jnp.concatenate([block[:, i * CHUNK:(i + 1) * CHUNK] for block in blocks], axis=0)
        loads[i].wait()
        total[...] += jnp.dot(rows, weight_buf[i], preferred_element_type=jnp.float32)


def first_kernel(*refs):
    total, weight_buf, sem = refs[-3:]
    total[...] = jnp.zeros_like(total)
    multiply(refs[:RING], refs[RING], 0, total, weight_buf, sem)


def project_first(blocks, weight):
    width, both = weight.shape
    rows = RING * blocks[0].shape[0]
    return pl.pallas_call(
        first_kernel,
        out_shape=jax.ShapeDtypeStruct((rows, both), jnp.float32),
        in_specs=[VMEM] * len(blocks) + [HBM],
        out_specs=VMEM,
        scratch_shapes=[
            pltpu.VMEM((width // 2 // CHUNK, CHUNK, both), jnp.bfloat16),
            pltpu.SemaphoreType.DMA((width // 2 // CHUNK,)),
        ],
        compiler_params=pltpu.CompilerParams(vmem_limit_bytes=48 * MIB),
        cost_estimate=pl.CostEstimate(flops=rows * width * both, bytes_accessed=width * both, transcendentals=0),
        name="project_first",
    )(*blocks, weight)


def project_kernel(info, gain, *refs):
    n = RING
    blocks, weight, first = refs[:n], refs[n], refs[n + 1]
    out, squares, query_total, weight_buf, total, raw, weight_sem = refs[-7:]
    width = weight.shape[0] // 2
    total[...] = first[...]
    multiply(blocks, weight, width, total, weight_buf, weight_sem)
    riders = [block[:, width:].astype(jnp.float32) for block in blocks]
    query_total[...] = sum(rider[:16] + rider[16:] for rider in riders)
    columns = out.shape[-1] // 2
    enc, seq = info[0], info[1]
    place = lax.broadcasted_iota(jnp.int32, (8, columns), 0)
    way = 1 - 2 * lax.rem(seq, 2)
    for i, offset in enumerate(PLANES):
        plane = lax.rem(enc + way * offset + RING, RING)
        for t in range(4):
            both = total[32 * i + 8 * t:32 * i + 8 * t + 8, :]
            live = plane * 64 + seq * 8 + place < info[2 + t]
            raw[t, plane] = both[:, :columns]
            out[t, plane, :, :columns] = (both[:, :columns] * gain[...][None, :]).astype(out.dtype)
            out[t, plane, :, columns:] = jnp.where(
                live, both[:, columns:] * V_DOWN, 0.0
            ).astype(out.dtype)
    square = raw[...].reshape(256, columns)
    square = square * square
    upper = square.astype(jnp.bfloat16)
    lower = (square - upper.astype(jnp.float32)).astype(jnp.bfloat16)
    ones = jnp.ones((8, columns), jnp.bfloat16)
    across = (((1,), (1,)), ((), ()))
    summed = lax.dot_general(
        ones, upper, across, preferred_element_type=jnp.float32
    ) + lax.dot_general(ones, lower, across, preferred_element_type=jnp.float32)
    for i in range(0, squares.shape[0], 8):
        squares[i:i + 8] = summed.reshape(8, 1, 256)


def project(info, gain, blocks, weight, first):
    width, both = weight.shape
    return pl.pallas_call(
        project_kernel,
        out_shape=(
            jax.ShapeDtypeStruct((4, 8, 8, both), jnp.bfloat16),
            jax.ShapeDtypeStruct((64, 1, 256), jnp.float32),
            jax.ShapeDtypeStruct((16, HD), jnp.float32),
        ),
        in_specs=[SMEM] + [VMEM] * (len(blocks) + 1) + [HBM, VMEM],
        out_specs=[VMEM] * 3,
        scratch_shapes=[
            pltpu.VMEM((width // 2 // CHUNK, CHUNK, both), jnp.bfloat16),
            pltpu.VMEM((256, both), jnp.float32),
            pltpu.VMEM((4, 8, 8, both // 2), jnp.float32),
            pltpu.SemaphoreType.DMA((width // 2 // CHUNK,)),
        ],
        compiler_params=pltpu.CompilerParams(vmem_limit_bytes=48 * MIB),
        cost_estimate=pl.CostEstimate(
            flops=256 * width * both, bytes_accessed=width * both, transcendentals=0
        ),
        name="project",
    )(info, gain, *blocks, weight, first)


def total_kernel(piece, squares, out, total):
    for i in range(8):
        row = squares[i]
        for plane in range(1, 8):
            row = row + squares[8 * plane + i]
        total[i:i + 1, :] = row


def key_sums(piece, squares):
    return pl.pallas_call(
        total_kernel,
        out_shape=(jax.ShapeDtypeStruct(piece.shape, piece.dtype), jax.ShapeDtypeStruct((8, 256), jnp.float32)),
        in_specs=[HBM, VMEM],
        out_specs=[HBM, VMEM],
        input_output_aliases={0: 0},
        compiler_params=pltpu.CompilerParams(vmem_limit_bytes=4 * MIB),
        name="key_sums",
    )(piece, squares)


def scale_kernel(width, queries, gain, query_total, out):
    scale = jnp.transpose(lax.rsqrt(query_total[...] / width + 1e-06))
    for f in range(queries.shape[0] // FRAME):
        rows = slice(f * FRAME, (f + 1) * FRAME)
        out[rows, :] = (
            queries[rows, :].astype(jnp.float32) * scale[:, f:f + 1] * gain[...][None, :] * HD ** (-0.5)
        ).astype(out.dtype)


def scale_queries(width, queries, gain, query_total):
    return pl.pallas_call(
        functools.partial(scale_kernel, width),
        out_shape=jax.ShapeDtypeStruct(queries.shape, queries.dtype),
        in_specs=[VMEM] * 3,
        out_specs=VMEM,
        compiler_params=pltpu.CompilerParams(vmem_limit_bytes=12 * MIB),
        name="scale_queries",
    )(queries, gain, query_total)


def attend_kernel(width, info, q_buf, key_total, *refs):
    parts, out = refs[:8], refs[8]
    o_buf, k_buf, v_buf, scale_buf, sem = refs[9:]
    seq, heads = info[1], q_buf.shape[1] // HD
    columns = heads * HD
    frames = q_buf.shape[0] // FRAME

    def piece_seq(piece):
        y, c = seq // 2, seq % 2
        kind = piece % 4
        shift = jnp.where(kind == 0, 0, jnp.where(kind == 1, 3, jnp.where(kind == 2, 1, 2)))
        return 2 * ((y + shift) % 4) + (c + piece // 4) % 2

    def position(shape, axis):
        key = lax.broadcasted_iota(jnp.int32, shape, axis)
        return key // 8 % 8 * 64 + piece_seq(key // 64) * 8 + key % 8

    down, across = position((512, HD), 0), position((1, 512), 1)
    totals = [key_total[pl.ds(piece_seq(p), 1), :] for p in range(8)]
    scales = [lax.rsqrt(total / width + 1e-06) * math.log2(math.e) for total in totals]
    for t in range(4):
        live = jnp.where(down < info[2 + t], 1.0, 0.0).astype(v_buf.dtype)
        row = jnp.concatenate([scale[:, t * 64:t * 64 + 64] for scale in scales], axis=1)
        scale_buf[t:t + 1, :] = jnp.where(across < info[2 + t], row, 0.0)
        for p in range(8):
            spot = slice(64 * p, 64 * p + 64)
            k_buf[t, spot, :] = parts[p][t, :, :columns]
            for h in range(heads):
                v_buf[h, t, spot, :HD] = parts[p][t, :, columns + h * HD:columns + (h + 1) * HD]
        for h in range(heads):
            v_buf[h, t, :, HD:] = live

    def frame_copy(f):
        rows = pl.ds(pl.multiple_of(f * FRAME, FRAME), FRAME)
        return pltpu.make_async_copy(o_buf.at[rows], out.at[rows], sem.at[f])

    for t in range(4):
        first, last = info[10 + t], info[11 + t]

        def one(i, carry, t=t, first=first, last=last):
            frame = first + GROUP * i
            base = jnp.minimum(frame, frames - GROUP)
            rows = pl.ds(pl.multiple_of(base * FRAME, FRAME), GROUP * FRAME)
            places = [
                pl.ds(pl.multiple_of(jnp.where(base + g < frame, frames, base + g) * FRAME, FRAME), FRAME)
                for g in range(GROUP)
            ]
            for h in range(heads):
                lanes = slice(h * HD, (h + 1) * HD)
                scores = lax.dot_general(
                    q_buf[rows, lanes], k_buf[t, :, lanes], (((1,), (1,)), ((), ())),
                    preferred_element_type=jnp.float32,
                )
                raised = jnp.exp2(scores * scale_buf[t:t + 1, :]).astype(jnp.bfloat16)
                mixed = jnp.dot(raised, v_buf[h, t], preferred_element_type=jnp.float32)
                result = (mixed[:, :HD] * (1.0 / mixed[:, HD:]) * (1.0 / V_DOWN)).astype(o_buf.dtype)
                for g, place in enumerate(places):
                    o_buf[place, lanes] = result[g * FRAME:(g + 1) * FRAME]
            for g in range(GROUP):

                @pl.when(frame + g < last)
                def _(g=g):
                    frame_copy(frame + g).start()

            return carry

        lax.fori_loop(0, (last - first + GROUP - 1) // GROUP, one, 0)
    for f in range(frames):
        frame_copy(f).wait()


def attend(width, info, queries, key_total, parts):
    rows, columns = queries.shape
    return pl.pallas_call(
        functools.partial(attend_kernel, width),
        out_shape=jax.ShapeDtypeStruct((rows, columns), queries.dtype),
        in_specs=[SMEM] + [VMEM] * 10,
        out_specs=HBM,
        scratch_shapes=[
            pltpu.VMEM((rows + FRAME, columns), queries.dtype),
            pltpu.VMEM((4, 512, columns), queries.dtype),
            pltpu.VMEM((columns // HD, 4, 512, 2 * HD), queries.dtype),
            pltpu.VMEM((8, 512), jnp.float32),
            pltpu.SemaphoreType.DMA((rows // FRAME,)),
        ],
        compiler_params=pltpu.CompilerParams(vmem_limit_bytes=20 * MIB),
        cost_estimate=pl.CostEstimate(flops=4 * rows * columns * 512, bytes_accessed=4 * rows * columns, transcendentals=0),
        name="attend",
    )(info, queries, key_total, *parts)


def local(queries, text, kv_weight, query_gain, key_gain, prompt_len, served, frame_slot):
    columns = queries.shape[1]
    full_width = columns * 8
    enc, rep, seq = (lax.axis_index(a) for a in ("enc", "rep", "seq"))
    mine = lax.dynamic_slice_in_dim(served, rep * 4, 4)
    code = (mine // 4 - rep + 4) % 4 * 4 + mine % 4
    bounds = jnp.sum(frame_slot.reshape(1, -1) < jnp.arange(5, dtype=jnp.int32)[:, None], axis=1, dtype=jnp.int32)
    info = jnp.concatenate([jnp.stack([enc, seq]).astype(jnp.int32), prompt_len[mine], code, bounds])
    query_float = queries.astype(jnp.float32)
    query_square = jnp.sum(query_float * query_float, axis=-1).reshape(-1, HD)
    weight = kv_weight.reshape(kv_weight.shape[0], 2 * columns)

    parts = [text] + [lax.ppermute(text, "rep", ring(4, k)) for k in (-1, 2, 1)]
    blocks = [picked.reshape(32, picked.shape[2]) for picked in pick(info, parts, query_square, weight)]

    ups, downs = [[b] for b in blocks], [[b] for b in blocks]
    for i in range(4):
        for n in range(2):
            if n == 0 or i < 3:
                ups[n].append(lax.ppermute(ups[n][-1], ("enc", "seq"), planes(1)))
            if n == 1 or i < 3:
                downs[n].append(lax.ppermute(downs[n][-1], ("enc", "seq"), planes(-1)))
    first = project_first(ups[0] + downs[0][1:], weight)
    held = ups[1] + [downs[1][4]] + downs[1][1:4]
    pair, squares, query_total = project(info, key_gain, held, weight, first)
    pair = pair.reshape(4, 64, 2 * columns)

    squares = lax.all_to_all(squares, ("enc", "seq"), 0, 0, tiled=True)
    ahead, behind, far = (lax.ppermute(pair, "seq", p) for p in (Y_UP, Y_DOWN, Y_FAR))
    far, key_total = key_sums(far, squares)
    parts = [pair, ahead, behind, far]
    parts = parts + [lax.ppermute(part, "seq", CORE) for part in parts]
    scaled = scale_queries(full_width, queries, query_gain, query_total)
    return attend(full_width, info, scaled, key_total, parts)


def solution(mesh):
    placed = (
        P(("rep", "seq"), "enc"),
        P("rep", ("enc", "seq"), None),
        P(None, None, "enc"),
        P("enc"),
        P("enc"),
        P(),
        P(),
        P("rep", "seq"),
    )
    return jax.shard_map(
        local, mesh=mesh, in_specs=placed, out_specs=P(("rep", "seq"), "enc"), check_vma=False
    )
```

```python
import functools
import math

import jax
import jax.numpy as jnp
from jax import lax
from jax.experimental import pallas as pl
from jax.experimental.pallas import tpu as pltpu
from jax.sharding import PartitionSpec as P

HD = 128
FRAME = 128
V_DOWN = 2.0 ** -12
MIB = 1024 * 1024
CHUNK = 512
GROUP = 4
RING = 8
PLANES = (0, -1, -2, -3, 4, 1, 2, 3)

SMEM = pl.BlockSpec(memory_space=pltpu.SMEM)
VMEM = pl.BlockSpec(memory_space=pltpu.VMEM)
HBM = pl.BlockSpec(memory_space=pl.ANY)


def ring(n, k):
    return [(i, (i + k) % n) for i in range(n)]


def planes(k):
    return [(i * 8 + s, (i + k * (1 - 2 * (s % 2))) % RING * 8 + s) for i in range(RING) for s in range(8)]


Y_UP = [(s, (s + 2) % 8) for s in range(8)]
Y_DOWN = [(s, (s - 2) % 8) for s in range(8)]
Y_FAR = [(s, (s + 4) % 8) for s in range(8)]
CORE = [(s, s ^ 1) for s in range(8)]


def pick_kernel(info, *refs):
    sources, square = refs[:4], refs[4]
    out_a, out_b, sem = refs[-3:]
    tenants, rows, width = out_a.shape
    copies = []
    for j in range(tenants):
        step, slot = info[6 + j] // 4, info[6 + j] % 4
        for n, target in enumerate((out_a.at[j], out_b.at[j, :, pl.ds(0, width)])):
            span = pl.ds(n * width, width)

            def send(source, index, target=target, span=span, j=j, n=n):
                pltpu.make_async_copy(source.at[index, :, span], target, sem.at[n, j]).start()

            for i, source in enumerate(sources):
                pl.when(step == i)(functools.partial(send, source, slot))
            copies.append(pltpu.make_async_copy(sources[0].at[0, :, span], target, sem.at[n, j]))
    for j in range(2):
        part = square[j * rows:(j + 1) * rows, :]
        upper = part.astype(out_b.dtype)
        out_b[j, :, width:] = upper
        out_b[2 + j, :, width:] = (part - upper.astype(jnp.float32)).astype(out_b.dtype)
    for copy in copies:
        copy.wait()


def pick(info, parts, square, weight):
    n, rows, width = parts[0].shape
    return pl.pallas_call(
        pick_kernel,
        out_shape=(
            jax.ShapeDtypeStruct((n, rows, width // 2), parts[0].dtype),
            jax.ShapeDtypeStruct((n, rows, width // 2 + HD), parts[0].dtype),
        ),
        in_specs=[SMEM] + [HBM] * 4 + [VMEM, HBM],
        out_specs=[VMEM] * 2,
        scratch_shapes=[pltpu.SemaphoreType.DMA((2, n))],
        compiler_params=pltpu.CompilerParams(vmem_limit_bytes=48 * MIB),
        name="pick",
    )(info, *parts, square, weight)


def multiply(blocks, weight, start, total, weight_buf, sem):
    steps = range(weight_buf.shape[0])
    loads = [
        pltpu.make_async_copy(weight.at[pl.ds(start + i * CHUNK, CHUNK)], weight_buf.at[i], sem.at[i])
        for i in steps
    ]
    for load in loads:
        load.start()
    for i in steps:
        rows = jnp.concatenate([block[:, i * CHUNK:(i + 1) * CHUNK] for block in blocks], axis=0)
        loads[i].wait()
        total[...] += jnp.dot(rows, weight_buf[i], preferred_element_type=jnp.float32)


def first_kernel(*refs):
    total, weight_buf, sem = refs[-3:]
    total[...] = jnp.zeros_like(total)
    multiply(refs[:RING], refs[RING], 0, total, weight_buf, sem)


def project_first(blocks, weight):
    width, both = weight.shape
    rows = RING * blocks[0].shape[0]
    return pl.pallas_call(
        first_kernel,
        out_shape=jax.ShapeDtypeStruct((rows, both), jnp.float32),
        in_specs=[VMEM] * len(blocks) + [HBM],
        out_specs=VMEM,
        scratch_shapes=[
            pltpu.VMEM((width // 2 // CHUNK, CHUNK, both), jnp.bfloat16),
            pltpu.SemaphoreType.DMA((width // 2 // CHUNK,)),
        ],
        compiler_params=pltpu.CompilerParams(vmem_limit_bytes=48 * MIB),
        cost_estimate=pl.CostEstimate(flops=rows * width * both, bytes_accessed=width * both, transcendentals=0),
        name="project_first",
    )(*blocks, weight)


def project_kernel(info, gain, *refs):
    n = RING
    blocks, weight, first = refs[:n], refs[n], refs[n + 1]
    out, squares, query_total, weight_buf, total, raw, weight_sem = refs[-7:]
    width = weight.shape[0] // 2
    total[...] = first[...]
    multiply(blocks, weight, width, total, weight_buf, weight_sem)
    riders = [block[:, width:].astype(jnp.float32) for block in blocks]
    query_total[...] = sum(rider[:16] + rider[16:] for rider in riders)
    columns = out.shape[-1] // 2
    enc, seq = info[0], info[1]
    place = lax.broadcasted_iota(jnp.int32, (8, columns), 0)
    way = 1 - 2 * lax.rem(seq, 2)
    for i, offset in enumerate(PLANES):
        plane = lax.rem(enc + way * offset + RING, RING)
        for t in range(4):
            both = total[32 * i + 8 * t:32 * i + 8 * t + 8, :]
            live = plane * 64 + seq * 8 + place < info[2 + t]
            raw[t, plane] = both[:, :columns]
            out[t, plane, :, :columns] = (both[:, :columns] * gain[...][None, :]).astype(out.dtype)
            out[t, plane, :, columns:] = jnp.where(
                live, both[:, columns:] * V_DOWN, 0.0
            ).astype(out.dtype)
    square = raw[...].reshape(256, columns)
    square = square * square
    upper = square.astype(jnp.bfloat16)
    lower = (square - upper.astype(jnp.float32)).astype(jnp.bfloat16)
    ones = jnp.ones((8, columns), jnp.bfloat16)
    across = (((1,), (1,)), ((), ()))
    summed = lax.dot_general(
        ones, upper, across, preferred_element_type=jnp.float32
    ) + lax.dot_general(ones, lower, across, preferred_element_type=jnp.float32)
    for i in range(0, squares.shape[0], 8):
        squares[i:i + 8] = summed.reshape(8, 1, 256)


def project(info, gain, blocks, weight, first):
    width, both = weight.shape
    return pl.pallas_call(
        project_kernel,
        out_shape=(
            jax.ShapeDtypeStruct((4, 8, 8, both), jnp.bfloat16),
            jax.ShapeDtypeStruct((32, 1, 256), jnp.float32),
            jax.ShapeDtypeStruct((16, HD), jnp.float32),
        ),
        in_specs=[SMEM] + [VMEM] * (len(blocks) + 1) + [HBM, VMEM],
        out_specs=[VMEM] * 3,
        scratch_shapes=[
            pltpu.VMEM((width // 2 // CHUNK, CHUNK, both), jnp.bfloat16),
            pltpu.VMEM((256, both), jnp.float32),
            pltpu.VMEM((4, 8, 8, both // 2), jnp.float32),
            pltpu.SemaphoreType.DMA((width // 2 // CHUNK,)),
        ],
        compiler_params=pltpu.CompilerParams(vmem_limit_bytes=48 * MIB),
        cost_estimate=pl.CostEstimate(
            flops=256 * width * both, bytes_accessed=width * both, transcendentals=0
        ),
        name="project",
    )(info, gain, *blocks, weight, first)


def total_kernel(piece, squares, out, total):
    for i in range(4):
        row = squares[i]
        for plane in range(1, 8):
            row = row + squares[4 * plane + i]
        total[i:i + 1, :] = row
        total[i + 4:i + 5, :] = row


def key_sums(piece, squares):
    return pl.pallas_call(
        total_kernel,
        out_shape=(jax.ShapeDtypeStruct(piece.shape, piece.dtype), jax.ShapeDtypeStruct((8, 256), jnp.float32)),
        in_specs=[HBM, VMEM],
        out_specs=[HBM, VMEM],
        input_output_aliases={0: 0},
        compiler_params=pltpu.CompilerParams(vmem_limit_bytes=4 * MIB),
        name="key_sums",
    )(piece, squares)


def scale_kernel(width, queries, gain, query_total, out):
    scale = jnp.transpose(lax.rsqrt(query_total[...] / width + 1e-06))
    for f in range(queries.shape[0] // FRAME):
        rows = slice(f * FRAME, (f + 1) * FRAME)
        out[rows, :] = (
            queries[rows, :].astype(jnp.float32) * scale[:, f:f + 1] * gain[...][None, :] * HD ** (-0.5)
        ).astype(out.dtype)


def scale_queries(width, queries, gain, query_total):
    return pl.pallas_call(
        functools.partial(scale_kernel, width),
        out_shape=jax.ShapeDtypeStruct(queries.shape, queries.dtype),
        in_specs=[VMEM] * 3,
        out_specs=VMEM,
        compiler_params=pltpu.CompilerParams(vmem_limit_bytes=6 * MIB),
        name="scale_queries",
    )(queries, gain, query_total)


def attend_kernel(width, info, q_buf, key_total, core_total, *refs):
    parts, out = refs[:8], refs[8]
    o_buf, k_buf, v_buf, scale_buf, sem = refs[9:]
    seq, heads = info[1], q_buf.shape[1] // HD
    columns = heads * HD
    frames = q_buf.shape[0] // FRAME

    def piece_seq(piece):
        y, c = seq // 2, seq % 2
        kind = piece % 4
        shift = jnp.where(kind == 0, 0, jnp.where(kind == 1, 3, jnp.where(kind == 2, 1, 2)))
        return 2 * ((y + shift) % 4) + (c + piece // 4) % 2

    def position(shape, axis):
        key = lax.broadcasted_iota(jnp.int32, shape, axis)
        return key // 8 % 8 * 64 + piece_seq(key // 64) * 8 + key % 8

    down, across = position((512, HD), 0), position((1, 512), 1)
    totals = [(core_total if p >= 4 else key_total)[pl.ds(piece_seq(p) // 2, 1), :] for p in range(8)]
    scales = [lax.rsqrt(total / width + 1e-06) * math.log2(math.e) for total in totals]
    for t in range(4):
        live = jnp.where(down < info[2 + t], 1.0, 0.0).astype(v_buf.dtype)
        row = jnp.concatenate([scale[:, t * 64:t * 64 + 64] for scale in scales], axis=1)
        scale_buf[t:t + 1, :] = jnp.where(across < info[2 + t], row, 0.0)
        for p in range(8):
            spot = slice(64 * p, 64 * p + 64)
            k_buf[t, spot, :] = parts[p][t, :, :columns]
            for h in range(heads):
                v_buf[h, t, spot, :HD] = parts[p][t, :, columns + h * HD:columns + (h + 1) * HD]
        for h in range(heads):
            v_buf[h, t, :, HD:] = live

    def frame_copy(f):
        rows = pl.ds(pl.multiple_of(f * FRAME, FRAME), FRAME)
        return pltpu.make_async_copy(o_buf.at[rows], out.at[rows], sem.at[f])

    for t in range(4):
        first, last = info[10 + t], info[11 + t]

        def one(i, carry, t=t, first=first, last=last):
            frame = first + GROUP * i
            base = jnp.minimum(frame, frames - GROUP)
            rows = pl.ds(pl.multiple_of(base * FRAME, FRAME), GROUP * FRAME)
            places = [
                pl.ds(pl.multiple_of(jnp.where(base + g < frame, frames, base + g) * FRAME, FRAME), FRAME)
                for g in range(GROUP)
            ]
            for h in range(heads):
                lanes = slice(h * HD, (h + 1) * HD)
                scores = lax.dot_general(
                    q_buf[rows, lanes], k_buf[t, :, lanes], (((1,), (1,)), ((), ())),
                    preferred_element_type=jnp.float32,
                )
                raised = jnp.exp2(scores * scale_buf[t:t + 1, :]).astype(jnp.bfloat16)
                mixed = jnp.dot(raised, v_buf[h, t], preferred_element_type=jnp.float32)
                result = (mixed[:, :HD] * (1.0 / mixed[:, HD:]) * (1.0 / V_DOWN)).astype(o_buf.dtype)
                for g, place in enumerate(places):
                    o_buf[place, lanes] = result[g * FRAME:(g + 1) * FRAME]
            for g in range(GROUP):

                @pl.when(frame + g < last)
                def _(g=g):
                    frame_copy(frame + g).start()

            return carry

        lax.fori_loop(0, (last - first + GROUP - 1) // GROUP, one, 0)
    for f in range(frames):
        frame_copy(f).wait()


def attend(width, info, queries, key_total, core_total, parts):
    rows, columns = queries.shape
    return pl.pallas_call(
        functools.partial(attend_kernel, width),
        out_shape=jax.ShapeDtypeStruct((rows, columns), queries.dtype),
        in_specs=[SMEM] + [VMEM] * 11,
        out_specs=HBM,
        scratch_shapes=[
            pltpu.VMEM((rows + FRAME, columns), queries.dtype),
            pltpu.VMEM((4, 512, columns), queries.dtype),
            pltpu.VMEM((columns // HD, 4, 512, 2 * HD), queries.dtype),
            pltpu.VMEM((8, 512), jnp.float32),
            pltpu.SemaphoreType.DMA((rows // FRAME,)),
        ],
        compiler_params=pltpu.CompilerParams(vmem_limit_bytes=12 * MIB),
        cost_estimate=pl.CostEstimate(flops=4 * rows * columns * 512, bytes_accessed=4 * rows * columns, transcendentals=0),
        name="attend",
    )(info, queries, key_total, core_total, *parts)


def local(queries, text, kv_weight, query_gain, key_gain, prompt_len, served, frame_slot):
    columns = queries.shape[1]
    full_width = columns * 8
    enc, rep, seq = (lax.axis_index(a) for a in ("enc", "rep", "seq"))
    mine = lax.dynamic_slice_in_dim(served, rep * 4, 4)
    code = (mine // 4 - rep + 4) % 4 * 4 + mine % 4
    bounds = jnp.sum(frame_slot.reshape(1, -1) < jnp.arange(5, dtype=jnp.int32)[:, None], axis=1, dtype=jnp.int32)
    info = jnp.concatenate([jnp.stack([enc, seq]).astype(jnp.int32), prompt_len[mine], code, bounds])
    query_float = queries.astype(jnp.float32)
    query_square = jnp.sum(query_float * query_float, axis=-1).reshape(-1, HD)
    weight = kv_weight.reshape(kv_weight.shape[0], 2 * columns)

    parts = [text] + [lax.ppermute(text, "rep", ring(4, k)) for k in (-1, 2, 1)]
    blocks = [picked.reshape(32, picked.shape[2]) for picked in pick(info, parts, query_square, weight)]

    ups, downs = [[b] for b in blocks], [[b] for b in blocks]
    for i in range(4):
        for n in range(2):
            if n == 0 or i < 3:
                ups[n].append(lax.ppermute(ups[n][-1], ("enc", "seq"), planes(1)))
            if n == 1 or i < 3:
                downs[n].append(lax.ppermute(downs[n][-1], ("enc", "seq"), planes(-1)))
    first = project_first(ups[0] + downs[0][1:], weight)
    held = ups[1] + [downs[1][4]] + downs[1][1:4]
    pair, squares, query_total = project(info, key_gain, held, weight, first)
    pair = pair.reshape(4, 64, 2 * columns)

    same_core = [[e * 8 + 2 * y + c for e in range(8) for y in range(4)] for c in range(2)]
    squares = lax.all_to_all(squares, ("enc", "seq"), 0, 0, axis_index_groups=same_core, tiled=True)
    ahead, behind, far = (lax.ppermute(pair, "seq", p) for p in (Y_UP, Y_DOWN, Y_FAR))
    far, key_total = key_sums(far, squares)
    parts = [pair, ahead, behind, far]
    parts = parts + [lax.ppermute(part, "seq", CORE) for part in parts]
    scaled = scale_queries(full_width, queries, query_gain, query_total)
    return attend(full_width, info, scaled, key_total, lax.ppermute(key_total, "seq", CORE), parts)


def solution(mesh):
    placed = (
        P(("rep", "seq"), "enc"),
        P("rep", ("enc", "seq"), None),
        P(None, None, "enc"),
        P("enc"),
        P("enc"),
        P(),
        P(),
        P("rep", "seq"),
    )
    return jax.shard_map(
        local, mesh=mesh, in_specs=placed, out_specs=P(("rep", "seq"), "enc"), check_vma=False
    )
```

```python
import functools
import math

import jax
import jax.numpy as jnp
from jax import lax
from jax.experimental import pallas as pl
from jax.experimental.pallas import tpu as pltpu
from jax.sharding import PartitionSpec as P

HD = 128
FRAME = 128
V_DOWN = 2.0 ** -12
MIB = 1024 * 1024
CHUNK = 1280
GROUP = 4
RING = 8
PLANES = (0, -1, -2, -3, 4, 1, 2, 3)

SMEM = pl.BlockSpec(memory_space=pltpu.SMEM)
VMEM = pl.BlockSpec(memory_space=pltpu.VMEM)
HBM = pl.BlockSpec(memory_space=pl.ANY)


def ring(n, k):
    return [(i, (i + k) % n) for i in range(n)]


def planes(k):
    return [(i * 8 + s, (i + k * (1 - 2 * (s % 2))) % RING * 8 + s) for i in range(RING) for s in range(8)]


Y_UP = [(s, (s + 2) % 8) for s in range(8)]
Y_DOWN = [(s, (s - 2) % 8) for s in range(8)]
Y_FAR = [(s, (s + 4) % 8) for s in range(8)]
CORE = [(s, s ^ 1) for s in range(8)]


def pick_kernel(info, *refs):
    sources, square = refs[:4], refs[4]
    out_a, out_b, sem = refs[-3:]
    tenants, rows, width = out_a.shape
    copies = []
    for j in range(tenants):
        step, slot = info[6 + j] // 4, info[6 + j] % 4
        for n, target in enumerate((out_a.at[j], out_b.at[j, :, pl.ds(0, width)])):
            span = pl.ds(n * width, width)

            def send(source, index, target=target, span=span, j=j, n=n):
                pltpu.make_async_copy(source.at[index, :, span], target, sem.at[n, j]).start()

            for i, source in enumerate(sources):
                pl.when(step == i)(functools.partial(send, source, slot))
            copies.append(pltpu.make_async_copy(sources[0].at[0, :, span], target, sem.at[n, j]))
    for j in range(2):
        part = square[j * rows:(j + 1) * rows, :]
        upper = part.astype(out_b.dtype)
        out_b[j, :, width:] = upper
        out_b[2 + j, :, width:] = (part - upper.astype(jnp.float32)).astype(out_b.dtype)
    for copy in copies:
        copy.wait()


def pick(info, parts, square, weight):
    n, rows, width = parts[0].shape
    return pl.pallas_call(
        pick_kernel,
        out_shape=(
            jax.ShapeDtypeStruct((n, rows, width // 2), parts[0].dtype),
            jax.ShapeDtypeStruct((n, rows, width // 2 + HD), parts[0].dtype),
        ),
        in_specs=[SMEM] + [HBM] * 4 + [VMEM, HBM],
        out_specs=[VMEM] * 2,
        scratch_shapes=[pltpu.SemaphoreType.DMA((2, n))],
        compiler_params=pltpu.CompilerParams(vmem_limit_bytes=48 * MIB),
        name="pick",
    )(info, *parts, square, weight)


def multiply(blocks, weight, start, total, weight_buf, sem):
    steps = range(weight_buf.shape[0])
    loads = [
        pltpu.make_async_copy(weight.at[pl.ds(start + i * CHUNK, CHUNK)], weight_buf.at[i], sem.at[i])
        for i in steps
    ]
    for load in loads:
        load.start()
    for i in steps:
        rows = jnp.concatenate([block[:, i * CHUNK:(i + 1) * CHUNK] for block in blocks], axis=0)
        loads[i].wait()
        total[...] += jnp.dot(rows, weight_buf[i], preferred_element_type=jnp.float32)


def first_kernel(*refs):
    total, weight_buf, sem = refs[-3:]
    total[...] = jnp.zeros_like(total)
    multiply(refs[:RING], refs[RING], 0, total, weight_buf, sem)


def project_first(blocks, weight):
    width, both = weight.shape
    rows = RING * blocks[0].shape[0]
    return pl.pallas_call(
        first_kernel,
        out_shape=jax.ShapeDtypeStruct((rows, both), jnp.float32),
        in_specs=[VMEM] * len(blocks) + [HBM],
        out_specs=VMEM,
        scratch_shapes=[
            pltpu.VMEM((width // 2 // CHUNK, CHUNK, both), jnp.bfloat16),
            pltpu.SemaphoreType.DMA((width // 2 // CHUNK,)),
        ],
        compiler_params=pltpu.CompilerParams(vmem_limit_bytes=48 * MIB),
        cost_estimate=pl.CostEstimate(flops=rows * width * both, bytes_accessed=width * both, transcendentals=0),
        name="project_first",
    )(*blocks, weight)


def project_kernel(info, gain, *refs):
    n = RING
    blocks, weight, first = refs[:n], refs[n], refs[n + 1]
    out, squares, query_total, weight_buf, total, raw, weight_sem = refs[-7:]
    width = weight.shape[0] // 2
    total[...] = first[...]
    multiply(blocks, weight, width, total, weight_buf, weight_sem)
    riders = [block[:, width:].astype(jnp.float32) for block in blocks]
    query_total[...] = sum(rider[:16] + rider[16:] for rider in riders)
    columns = out.shape[-1] // 2
    enc, seq = info[0], info[1]
    place = lax.broadcasted_iota(jnp.int32, (8, columns), 0)
    way = 1 - 2 * lax.rem(seq, 2)
    for i, offset in enumerate(PLANES):
        plane = lax.rem(enc + way * offset + RING, RING)
        for t in range(4):
            both = total[32 * i + 8 * t:32 * i + 8 * t + 8, :]
            live = plane * 64 + seq * 8 + place < info[2 + t]
            raw[t, plane] = both[:, :columns]
            out[t, plane, :, :columns] = (both[:, :columns] * gain[...][None, :]).astype(out.dtype)
            out[t, plane, :, columns:] = jnp.where(
                live, both[:, columns:] * V_DOWN, 0.0
            ).astype(out.dtype)
    square = raw[...].reshape(256, columns)
    square = square * square
    upper = square.astype(jnp.bfloat16)
    lower = (square - upper.astype(jnp.float32)).astype(jnp.bfloat16)
    ones = jnp.ones((8, columns), jnp.bfloat16)
    across = (((1,), (1,)), ((), ()))
    summed = lax.dot_general(
        ones, upper, across, preferred_element_type=jnp.float32
    ) + lax.dot_general(ones, lower, across, preferred_element_type=jnp.float32)
    for i in range(0, squares.shape[0], 8):
        squares[i:i + 8] = summed.reshape(8, 1, 256)


def project(info, gain, blocks, weight, first):
    width, both = weight.shape
    return pl.pallas_call(
        project_kernel,
        out_shape=(
            jax.ShapeDtypeStruct((4, 8, 8, both), jnp.bfloat16),
            jax.ShapeDtypeStruct((32, 1, 256), jnp.float32),
            jax.ShapeDtypeStruct((16, HD), jnp.float32),
        ),
        in_specs=[SMEM] + [VMEM] * (len(blocks) + 1) + [HBM, VMEM],
        out_specs=[VMEM] * 3,
        scratch_shapes=[
            pltpu.VMEM((width // 2 // CHUNK, CHUNK, both), jnp.bfloat16),
            pltpu.VMEM((256, both), jnp.float32),
            pltpu.VMEM((4, 8, 8, both // 2), jnp.float32),
            pltpu.SemaphoreType.DMA((width // 2 // CHUNK,)),
        ],
        compiler_params=pltpu.CompilerParams(vmem_limit_bytes=48 * MIB),
        cost_estimate=pl.CostEstimate(
            flops=256 * width * both, bytes_accessed=width * both, transcendentals=0
        ),
        name="project",
    )(info, gain, *blocks, weight, first)


def total_kernel(piece, squares, out, total):
    for i in range(4):
        row = squares[i]
        for plane in range(1, 8):
            row = row + squares[4 * plane + i]
        total[i:i + 1, :] = row
        total[i + 4:i + 5, :] = row


def key_sums(piece, squares):
    return pl.pallas_call(
        total_kernel,
        out_shape=(jax.ShapeDtypeStruct(piece.shape, piece.dtype), jax.ShapeDtypeStruct((8, 256), jnp.float32)),
        in_specs=[HBM, VMEM],
        out_specs=[HBM, VMEM],
        input_output_aliases={0: 0},
        compiler_params=pltpu.CompilerParams(vmem_limit_bytes=4 * MIB),
        name="key_sums",
    )(piece, squares)


def scale_kernel(width, queries, gain, query_total, out):
    scale = jnp.transpose(lax.rsqrt(query_total[...] / width + 1e-06))
    for f in range(queries.shape[0] // FRAME):
        rows = slice(f * FRAME, (f + 1) * FRAME)
        out[rows, :] = (
            queries[rows, :].astype(jnp.float32) * scale[:, f:f + 1] * gain[...][None, :] * HD ** (-0.5)
        ).astype(out.dtype)


def scale_queries(width, queries, gain, query_total):
    return pl.pallas_call(
        functools.partial(scale_kernel, width),
        out_shape=jax.ShapeDtypeStruct(queries.shape, queries.dtype),
        in_specs=[VMEM] * 3,
        out_specs=VMEM,
        compiler_params=pltpu.CompilerParams(vmem_limit_bytes=6 * MIB),
        name="scale_queries",
    )(queries, gain, query_total)


def attend_kernel(width, info, q_buf, key_total, core_total, *refs):
    parts, out = refs[:8], refs[8]
    o_buf, k_buf, v_buf, scale_buf, sem = refs[9:]
    seq, heads = info[1], q_buf.shape[1] // HD
    columns = heads * HD
    frames = q_buf.shape[0] // FRAME

    def piece_seq(piece):
        y, c = seq // 2, seq % 2
        kind = piece % 4
        shift = jnp.where(kind == 0, 0, jnp.where(kind == 1, 3, jnp.where(kind == 2, 1, 2)))
        return 2 * ((y + shift) % 4) + (c + piece // 4) % 2

    def position(shape, axis):
        key = lax.broadcasted_iota(jnp.int32, shape, axis)
        return key // 8 % 8 * 64 + piece_seq(key // 64) * 8 + key % 8

    down, across = position((512, HD), 0), position((1, 512), 1)
    totals = [(core_total if p >= 4 else key_total)[pl.ds(piece_seq(p) // 2, 1), :] for p in range(8)]
    scales = [lax.rsqrt(total / width + 1e-06) * math.log2(math.e) for total in totals]
    for t in range(4):
        live = jnp.where(down < info[2 + t], 1.0, 0.0).astype(v_buf.dtype)
        row = jnp.concatenate([scale[:, t * 64:t * 64 + 64] for scale in scales], axis=1)
        scale_buf[t:t + 1, :] = jnp.where(across < info[2 + t], row, 0.0)
        for p in range(8):
            spot = slice(64 * p, 64 * p + 64)
            k_buf[t, spot, :] = parts[p][t, :, :columns]
            for h in range(heads):
                v_buf[h, t, spot, :HD] = parts[p][t, :, columns + h * HD:columns + (h + 1) * HD]
        for h in range(heads):
            v_buf[h, t, :, HD:] = live

    def frame_copy(f):
        rows = pl.ds(pl.multiple_of(f * FRAME, FRAME), FRAME)
        return pltpu.make_async_copy(o_buf.at[rows], out.at[rows], sem.at[f])

    for t in range(4):
        first, last = info[10 + t], info[11 + t]

        def one(i, carry, t=t, first=first, last=last):
            frame = first + GROUP * i
            base = jnp.minimum(frame, frames - GROUP)
            rows = pl.ds(pl.multiple_of(base * FRAME, FRAME), GROUP * FRAME)
            places = [
                pl.ds(pl.multiple_of(jnp.where(base + g < frame, frames, base + g) * FRAME, FRAME), FRAME)
                for g in range(GROUP)
            ]
            for h in range(heads):
                lanes = slice(h * HD, (h + 1) * HD)
                scores = lax.dot_general(
                    q_buf[rows, lanes], k_buf[t, :, lanes], (((1,), (1,)), ((), ())),
                    preferred_element_type=jnp.float32,
                )
                raised = jnp.exp2(scores * scale_buf[t:t + 1, :]).astype(jnp.bfloat16)
                mixed = jnp.dot(raised, v_buf[h, t], preferred_element_type=jnp.float32)
                result = (mixed[:, :HD] * (1.0 / mixed[:, HD:]) * (1.0 / V_DOWN)).astype(o_buf.dtype)
                for g, place in enumerate(places):
                    o_buf[place, lanes] = result[g * FRAME:(g + 1) * FRAME]
            for g in range(GROUP):

                @pl.when(frame + g < last)
                def _(g=g):
                    frame_copy(frame + g).start()

            return carry

        lax.fori_loop(0, (last - first + GROUP - 1) // GROUP, one, 0)
    for f in range(frames):
        frame_copy(f).wait()


def attend(width, info, queries, key_total, core_total, parts):
    rows, columns = queries.shape
    return pl.pallas_call(
        functools.partial(attend_kernel, width),
        out_shape=jax.ShapeDtypeStruct((rows, columns), queries.dtype),
        in_specs=[SMEM] + [VMEM] * 11,
        out_specs=HBM,
        scratch_shapes=[
            pltpu.VMEM((rows + FRAME, columns), queries.dtype),
            pltpu.VMEM((4, 512, columns), queries.dtype),
            pltpu.VMEM((columns // HD, 4, 512, 2 * HD), queries.dtype),
            pltpu.VMEM((8, 512), jnp.float32),
            pltpu.SemaphoreType.DMA((rows // FRAME,)),
        ],
        compiler_params=pltpu.CompilerParams(vmem_limit_bytes=12 * MIB),
        cost_estimate=pl.CostEstimate(flops=4 * rows * columns * 512, bytes_accessed=4 * rows * columns, transcendentals=0),
        name="attend",
    )(info, queries, key_total, core_total, *parts)


def local(queries, text, kv_weight, query_gain, key_gain, prompt_len, served, frame_slot):
    columns = queries.shape[1]
    full_width = columns * 8
    enc, rep, seq = (lax.axis_index(a) for a in ("enc", "rep", "seq"))
    mine = lax.dynamic_slice_in_dim(served, rep * 4, 4)
    code = (mine // 4 - rep + 4) % 4 * 4 + mine % 4
    bounds = jnp.sum(frame_slot.reshape(1, -1) < jnp.arange(5, dtype=jnp.int32)[:, None], axis=1, dtype=jnp.int32)
    info = jnp.concatenate([jnp.stack([enc, seq]).astype(jnp.int32), prompt_len[mine], code, bounds])
    query_float = queries.astype(jnp.float32)
    query_square = jnp.sum(query_float * query_float, axis=-1).reshape(-1, HD)
    weight = kv_weight.reshape(kv_weight.shape[0], 2 * columns)

    parts = [text] + [lax.ppermute(text, "rep", ring(4, k)) for k in (-1, 2, 1)]
    blocks = [picked.reshape(32, picked.shape[2]) for picked in pick(info, parts, query_square, weight)]

    ups, downs = [[b] for b in blocks], [[b] for b in blocks]
    for i in range(4):
        for n in range(2):
            if n == 0 or i < 3:
                ups[n].append(lax.ppermute(ups[n][-1], ("enc", "seq"), planes(1)))
            if n == 1 or i < 3:
                downs[n].append(lax.ppermute(downs[n][-1], ("enc", "seq"), planes(-1)))
    first = project_first(ups[0] + downs[0][1:], weight)
    held = ups[1] + [downs[1][4]] + downs[1][1:4]
    pair, squares, query_total = project(info, key_gain, held, weight, first)
    pair = pair.reshape(4, 64, 2 * columns)

    same_core = [[e * 8 + 2 * y + c for e in range(8) for y in range(4)] for c in range(2)]
    squares = lax.all_to_all(squares, ("enc", "seq"), 0, 0, axis_index_groups=same_core, tiled=True)
    ahead, behind, far = (lax.ppermute(pair, "seq", p) for p in (Y_UP, Y_DOWN, Y_FAR))
    far, key_total = key_sums(far, squares)
    parts = [pair, ahead, behind, far]
    parts = parts + [lax.ppermute(part, "seq", CORE) for part in parts]
    scaled = scale_queries(full_width, queries, query_gain, query_total)
    return attend(full_width, info, scaled, key_total, lax.ppermute(key_total, "seq", CORE), parts)


def solution(mesh):
    placed = (
        P(("rep", "seq"), "enc"),
        P("rep", ("enc", "seq"), None),
        P(None, None, "enc"),
        P("enc"),
        P("enc"),
        P(),
        P(),
        P("rep", "seq"),
    )
    return jax.shard_map(
        local, mesh=mesh, in_specs=placed, out_specs=P(("rep", "seq"), "enc"), check_vma=False
    )
```
